256 devices in a mesh: seg: 16 (over x_lo, z), head: 8 (over y, core), section: 2 (over x_hi).
Axes of the slice: x: 4 (x_hi: 2, x_lo: 2; x = x_hi * 2 + x_lo), y: 4, z: 8, core: 2. Of those that a mesh axis runs over, the one named last changes fastest.
Arguments:
- tokens: bfloat16 [3072, 3072], P('seg', 'head'), may hold values from -6 to 6
- in_weight: bfloat16 [2, 3, 3072, 3072], P('section', None, None, 'head'), may hold values from -0.109375 to 0.109375
- out_weight: bfloat16 [2, 3072, 3072], P('section', 'head'), may hold values from -0.109375 to 0.109375
- expand_init: float32 [2, 2, 48, 64, 128], P('section', None, 'head'), may hold values from -0.75 to 0.75
- contract_init: float32 [2, 2, 48, 128, 64], P('section', None, 'head'), may hold values from -0.5 to 0.5
- inner_rate: float32 [2, 2, 48], P('section', None, 'head'), may hold values from 0.1 to 1
- seg_counts: int32 [16], P('seg'), may hold values from 1 to 192, 2304 in all
Outputs:
- panels: bfloat16 [2, 3072, 3072], P('section', 'seg', 'head')
The draws below stay inside these ranges and needn't reach their ends.
Inputs may be any that keep to these rules, and one draw needn't show every extreme that they name: The live tokens of segment s are its first seg_counts[s]; the counts sum to 2304 and the largest equals 192.
All inputs are finite; a program needn't handle non-finite values. No bound on the sum of `seg_counts` on one device may be relied on, other than what follows from the above.
Results may differ from the reference program's by a relative error of at most 0.027.
Values may be sent and summed in bfloat16 or wider, within the bound.
A program may use at most 128 MiB of HBM per device.

```python
import math
import jax
import jax.numpy as jnp
import numpy as np
from jax import lax

D = 3072
HEADS = 48
HDIM = 64
FAST_WIDTH = 128
MB = 64
TOK_DEV = 192
TOKENS = 3072
N_SEG = 16
N_SECTION = 2


def levels(stream_key, extent, shards, low, largest):
    loudness = 1.0
    for axis_at, shards_of in shards:
        draws = jax.random.uniform(jax.random.fold_in(jax.random.fold_in(stream_key, 6), axis_at), (shards_of,), jnp.float32, low / len(shards), largest / len(shards))
        loudness = loudness * jnp.repeat(jnp.exp(draws), extent[axis_at] // shards_of).reshape((-1,) + (1,) * (len(extent) - 1 - axis_at))
    return loudness


def split_up(amount, total, most, skew):
    loads = [(1 << 20) // math.isqrt(grade ** skew) + 1 for grade in range(2, amount + 1)]
    surplus, given = total - most - (amount - 1), [1] * (amount - 1)
    while surplus > 0:
        movable = [i for i in range(amount - 1) if given[i] < most]
        mass, budget = sum([loads[i] for i in movable]), surplus
        for i in movable:
            addition = min(most - given[i], max(1, budget * loads[i] // mass), surplus)
            given[i] = given[i] + addition
            surplus = surplus - addition
    return np.array([most] + given)


def uneven(own_key, amount, total, reach, lean):
    if amount == 2:
        one = jax.random.randint(own_key, (), max(1, total - reach), min(reach, total - 1) + 1)
        return jnp.stack([one, total - one])
    sizes = jnp.asarray(split_up(amount, total, reach, lean), jnp.int32)
    couples = (amount - 1) // 2
    donor, receiver = sizes[1:1 + 2 * couples:2], sizes[2:2 + 2 * couples:2]
    margin = jnp.minimum(donor - 1, reach - receiver)
    passed = jax.random.randint(jax.random.fold_in(own_key, 1), (couples,), 0, 1 << 20) % (margin + 1)
    sizes = sizes.at[1:1 + 2 * couples:2].set(donor - passed).at[2:2 + 2 * couples:2].set(receiver + passed)
    return sizes[jax.random.permutation(jax.random.fold_in(own_key, 2), amount)]


def gaussian(rng, extent, scale, limit, shards=(), kind=jnp.bfloat16):
    drawn = scale * jax.random.normal(rng, extent, jnp.float32)
    if shards:
        drawn = drawn * levels(rng, extent, shards, -0.22, 0.18)
    return jnp.clip(drawn, -limit, limit).astype(kind)


def setup_inputs(seed: int = 0) -> dict:
    seeds = jax.random.split(jax.random.key(seed), 8)
    return {
        "tokens": gaussian(seeds[0], (TOKENS, D), 1.0, 6.0, ((0, 16), (1, 8))),
        "in_weight": gaussian(seeds[1], (N_SECTION, 3, D, HEADS * HDIM), D ** -0.5, 0.109375, ((0, 2), (3, 8))),
        "out_weight": gaussian(seeds[2], (N_SECTION, HEADS * HDIM, D), (HEADS * HDIM) ** -0.5, 0.109375, ((0, 2), (1, 8))),
        "expand_init": gaussian(seeds[3], (N_SECTION, 2, HEADS, HDIM, FAST_WIDTH), HDIM ** -0.5, 0.75, ((0, 2), (2, 8)), jnp.float32),
        "contract_init": gaussian(seeds[4], (N_SECTION, 2, HEADS, FAST_WIDTH, HDIM), FAST_WIDTH ** -0.5, 0.5, ((0, 2), (2, 8)), jnp.float32),
        "inner_rate": jnp.clip(jnp.exp(math.log(1.0) - 2.3025851 * jax.random.uniform(seeds[5], (N_SECTION, 2, HEADS), jnp.float32) ** levels(seeds[5], (N_SECTION, 2, HEADS), ((0, 2), (2, 8)), -0.2, 0.2)), 0.1, 1.0),
        "seg_counts": uneven(seeds[6], N_SEG, TOKENS * 3 // 4, TOK_DEV, 1).astype(jnp.int32),
    }


highest = lax.Precision.HIGHEST
gelu_coef = math.sqrt(2.0 / math.pi)
cubic_coef = 0.044715

def smooth(preact):
    return 0.5 * preact * (1.0 + jnp.tanh(gelu_coef * (preact + cubic_coef * preact * preact * preact)))

def slope(preact):
    curved = jnp.tanh(gelu_coef * (preact + cubic_coef * preact * preact * preact))
    return 0.5 * (1.0 + curved) + 0.5 * preact * (1.0 - curved * curved) * gelu_coef * (1.0 + 3.0 * cubic_coef * preact * preact)

def rescale(rows):
    return rows * lax.rsqrt(lax.optimization_barrier(jnp.mean(rows * rows, axis=-1, keepdims=True)) + 1e-06)

def inner_step(state, key_rows, value_rows, query_rows, live_rows, rate):
    batch_rows = key_rows.shape[0]
    step_rate = rate / key_rows.shape[2]
    preact = jnp.einsum('mhe,hef->mhf', key_rows, state[0], precision=highest)
    active = smooth(preact)
    predicted = key_rows + jnp.einsum('mhf,hef->mhe', active, state[1], precision=highest)
    misfit = (predicted - value_rows) * (live_rows / batch_rows)[:, None, None]
    backflow = jnp.einsum('mhe,hef->mhf', misfit, state[1], precision=highest) * slope(preact)
    grad_expand = jnp.einsum('mhe,mhf->hef', key_rows, backflow, precision=highest)
    grad_contract = jnp.einsum('mhe,mhf->hef', misfit, active, precision=highest)
    updated = state - step_rate[None, :, None, None] * jnp.stack([grad_expand, grad_contract])
    lifted = smooth(jnp.einsum('mhe,hef->mhf', query_rows, updated[0], precision=highest))
    result = query_rows + jnp.einsum('mhf,hef->mhe', lifted, updated[1], precision=highest)
    return (updated, result)

def run_blocks(state, key_all, value_all, query_all, live_all, rate, backward):

    def step(carry, pieces):
        return inner_step(carry, pieces[0], pieces[1], pieces[2], pieces[3], rate)
    final, results = lax.scan(step, state, (key_all, value_all, query_all, live_all), reverse=backward)
    return (final, results)

def layer(hidden, in_w, out_w, expand, contract, rates, live_mask):
    row_count = hidden.shape[0]
    head_count = expand.shape[1]
    head_width = expand.shape[2]
    blocks = row_count // MB

    def project(column):
        projected = jnp.dot(hidden, in_w[column], preferred_element_type=jnp.float32).astype(jnp.bfloat16)
        projected = lax.optimization_barrier(projected)
        return projected.astype(jnp.float32).reshape(blocks, MB, head_count, head_width)
    query_all = rescale(project(0))
    key_all = rescale(project(1))
    value_all = rescale(project(2))
    live_all = live_mask.reshape(blocks, MB)
    results = []
    for direction in range(2):
        state = jnp.stack([expand[direction], jnp.swapaxes(contract[direction], 1, 2)])
        final, result = run_blocks(state, key_all, value_all, query_all, live_all, rates[direction], direction == 1)
        results.append(result)
    mixture = (results[0] + results[1]).reshape(row_count, head_count * head_width).astype(jnp.bfloat16)
    summed = jnp.dot(mixture, out_w, preferred_element_type=jnp.float32)
    return (hidden.astype(jnp.float32) + summed).astype(jnp.bfloat16)

def reference(tokens, in_weight, out_weight, expand_init, contract_init, inner_rate, seg_counts):
    position = jnp.arange(TOKENS, dtype=jnp.int32)
    segment = (position // TOK_DEV).astype(jnp.int32)
    live_mask = (position % TOK_DEV < seg_counts[segment]).astype(jnp.float32)
    hidden = tokens
    panels = []
    for section_at in range(N_SECTION):
        hidden = layer(hidden, in_weight[section_at], out_weight[section_at], expand_init[section_at], contract_init[section_at], inner_rate[section_at], live_mask)
        panels.append(hidden)
    return jnp.stack(panels)
```

```python
import functools
import math

import jax
import jax.numpy as jnp
from jax import lax
from jax.experimental import pallas as pl
from jax.experimental.pallas import tpu as pltpu
from jax.sharding import PartitionSpec as P

MB = 64
C1 = math.sqrt(2.0 / math.pi)
C3 = 0.044715
f32 = jnp.float32
bf = jnp.bfloat16


def dot(a, b):
    return lax.dot_general(a, b, (((1,), (0,)), ((), ())), preferred_element_type=f32)


def dot_nt(a, b):
    return lax.dot_general(a, b, (((1,), (1,)), ((), ())), preferred_element_type=f32)


def dot_tn(a, b):
    return lax.dot_general(a, b, (((0,), (0,)), ((), ())), preferred_element_type=f32)


def smooth(z):
    t = jnp.tanh(z * (C1 + (C1 * C3) * (z * z)))
    h = 0.5 * z
    return h + h * t


def smooth_slope(z):
    z2 = z * z
    t = jnp.tanh(z * (C1 + (C1 * C3) * z2))
    h = 0.5 * z
    return h + h * t, 0.5 + 0.5 * t + h * (1.0 - t * t) * (C1 + (3.0 * C1 * C3) * z2)


def chain_kernel(nb, q, k, v, km, scale, u0, w0, o, u, w):
    u[...] = u0[...]
    w[...] = w0[...]

    def step(b, z):
        kb, kn, kmb, qb = k[b], k[jnp.minimum(b + 1, nb - 1)], km[b], q[b]
        a, s = smooth_slope(z)
        ab = a.astype(bf)
        wb = w[...].astype(bf)
        e = (kb.astype(f32) - v[b].astype(f32)) + dot_nt(ab, wb)
        back = (dot(e.astype(bf), wb) * s).astype(bf)
        ahead = dot(kn, u[...].astype(bf))
        gram = dot_nt(kn, kmb).astype(bf)
        z_next = ahead - dot(gram, back)
        un = u[...] - dot_tn(kmb, back)
        u[...] = un
        wn = w[...] - dot_tn((e * scale[b]).astype(bf), ab)
        w[...] = wn
        lifted = smooth(dot(qb, un.astype(bf))).astype(bf)
        o[b] = qb.astype(f32) + dot_nt(lifted, wn.astype(bf))
        return z_next

    lax.fori_loop(0, nb, step, dot(k[0], u0[...].astype(bf)))


def run_chain(q, k, v, km, scale, u0, w0):
    nb = q.shape[0]
    vm = pl.BlockSpec(memory_space=pltpu.VMEM)
    return pl.pallas_call(
        functools.partial(chain_kernel, nb),
        out_shape=jax.ShapeDtypeStruct(q.shape, f32),
        in_specs=[vm] * 7,
        out_specs=vm,
        scratch_shapes=[pltpu.VMEM(u0.shape, f32), pltpu.VMEM(w0.shape, f32)],
        compiler_params=pltpu.CompilerParams(vmem_limit_bytes=40 << 20),
        name="chain",
    )(q, k, v, km, scale, u0, w0)


def rescale(rows):
    return rows * lax.rsqrt(jnp.mean(rows * rows, axis=-1, keepdims=True) + 1e-06)


def layer(hidden, weights):
    in_w, out_rows, expand, contract, rates, live = weights
    n_seg = lax.axis_size("seg")
    heads, width = expand.shape[1], expand.shape[2]
    rows = hidden.shape[0]
    projected = jnp.einsum(
        "td,jdc->tjc",
        lax.all_gather(hidden, "head", axis=1, tiled=True),
        in_w,
        preferred_element_type=f32,
    )
    rounded = lax.optimization_barrier(projected.astype(bf)).astype(f32)
    unit = rescale(rounded.reshape(rows, 3, heads, width)).astype(bf)
    pieces = jnp.transpose(unit, (2, 0, 1, 3)).reshape(heads, rows, 3 * width)
    pieces = jnp.repeat(pieces, 2, axis=0)
    pieces = jnp.concatenate([pieces, pieces[: n_seg - 2 * heads]], axis=0)
    got = lax.all_to_all(pieces, "seg", 0, 0, tiled=True)
    blocks = n_seg * rows // MB
    me = lax.rem(lax.axis_index("seg"), 2 * heads)
    head, way = me // 2, lax.rem(me, 2)
    got = got.reshape(blocks, MB, 3 * width)
    mask = live.reshape(blocks, MB, 1)
    got = jnp.where(way == 1, got[::-1], got)
    mask = jnp.where(way == 1, mask[::-1], mask)
    q, k, v = got[..., :width], got[..., width : 2 * width], got[..., 2 * width :]
    scale = mask * (rates[way, head] / (width * MB))
    km = (k.astype(f32) * scale).astype(bf)
    out = run_chain(
        q,
        k,
        v,
        km,
        jnp.broadcast_to(scale, q.shape),
        expand[way, head],
        jnp.swapaxes(contract[way, head], 0, 1),
    )
    out = jnp.where(way == 1, out[::-1], out).astype(bf)
    back = lax.all_to_all(out.reshape(n_seg, rows, width), "seg", 0, 0, tiled=True)
    back = back[: 2 * heads].reshape(heads, 2, rows, width).astype(f32)
    mixture = jnp.swapaxes(back[:, 0] + back[:, 1], 0, 1).reshape(rows, heads * width).astype(bf)
    term = jnp.dot(mixture, out_rows, preferred_element_type=f32)
    summed = lax.psum_scatter(term.astype(bf), "head", scatter_dimension=1, tiled=True).astype(f32)
    return (hidden.astype(f32) + summed).astype(bf)


def local(tokens, in_weight, out_weight, expand_init, contract_init, inner_rate, seg_counts):
    counts = lax.all_gather(seg_counts, "seg", axis=0, tiled=True)
    position = lax.broadcasted_iota(jnp.int32, (counts.shape[0], tokens.shape[0]), 1)
    live = (position < counts[:, None]).astype(f32)
    weights = (in_weight[0], out_weight[0], expand_init[0], contract_init[0], inner_rate[0], live)
    earlier = layer(tokens, weights)
    n = lax.axis_size("section")
    handed = lax.ppermute(earlier, "section", [(i, i + 1) for i in range(n - 1)])
    later = layer(handed, weights)
    panel = jnp.where(lax.axis_index("section") == 0, earlier, later)
    return panel[None]


def solution(mesh):
    placed = (
        P("seg", "head"),
        P("section", None, None, "head"),
        P("section", "head", None),
        P("section", None, "head", None, None),
        P("section", None, "head", None, None),
        P("section", None, "head"),
        P("seg"),
    )
    return jax.shard_map(
        local, mesh=mesh, in_specs=placed, out_specs=P("section", "seg", "head"), check_vma=False
    )
```

```python
import functools
import math

import jax
import jax.numpy as jnp
from jax import lax
from jax.experimental import pallas as pl
from jax.experimental.pallas import tpu as pltpu
from jax.sharding import PartitionSpec as P

MB = 64
C1 = math.sqrt(2.0 / math.pi)
C3 = 0.044715
f32 = jnp.float32
bf = jnp.bfloat16


def dot(a, b):
    return lax.dot_general(a, b, (((1,), (0,)), ((), ())), preferred_element_type=f32)


def dot_nt(a, b):
    return lax.dot_general(a, b, (((1,), (1,)), ((), ())), preferred_element_type=f32)


def dot_tn(a, b):
    return lax.dot_general(a, b, (((0,), (0,)), ((), ())), preferred_element_type=f32)


def smooth(z):
    t = jnp.tanh(z * (C1 + (C1 * C3) * (z * z)))
    h = 0.5 * z
    return h + h * t


def smooth_slope(z):
    z2 = z * z
    t = jnp.tanh(z * (C1 + (C1 * C3) * z2))
    h = 0.5 * z
    return h + h * t, 0.5 + 0.5 * t + h * (1.0 - t * t) * (C1 + (3.0 * C1 * C3) * z2)


def chain_step(xl, bp, b, bn, z, bk, sc, u, w, ub, wk):
    xp, xb, xn = xl[bp, 0:64], xl[b, 0:64], xl[bn, 0:64]
    dp = xl[b, 64:96].astype(f32)
    hi = lax.broadcasted_iota(jnp.int32, (64, 128), 1) >= 64
    a, s = smooth_slope(z)
    s = s * sc
    ab = a.astype(bf)
    wkv = wk[...]
    p = dot_nt(ab, wkv)
    un = u[...] - dot_tn(xp, bk)[64:128]
    u[...] = un
    ub[64:128] = un.astype(bf)
    zu = dot(xn, ub[0:128])
    zq = dot(xp, ub[64:192])
    delta = jnp.where(hi, jnp.concatenate([pltpu.roll(dp, 64, 1), dp], 0), 0.0)
    e = delta + p
    f = dot(e.astype(bf), wkv)
    back = (f * s).astype(bf)
    gram = dot_nt(jnp.where(hi, xn, jnp.zeros_like(xn)), xb).astype(bf)
    zn = zu - dot(gram, back)
    aq = smooth(zq).astype(bf)
    out = pltpu.roll(xp.astype(f32), 64, 1) + dot_nt(aq, wkv)
    wn = w[...] - dot_tn((e * sc).astype(bf), ab)[64:128]
    w[...] = wn
    wk[64:128] = wn.astype(bf)
    return zn, back, out


def kernel(
    n_seg, n_head, heads,
    tokens, in_w, out_w, expand, contract, rate, counts,
    panel,
    inw, outw, hbuf, stg, xl, ini_s, ini, craw, exs, exl, mxs, mixb,
    p1, p2f, rs1, p2, rs2, u, w, ub, wk,
    wsem, tsem, isem, ag_s, ag_r, hop_s, hop_r, push_s, ch_r, fw_s, ex_s, ex_r,
    mix_s, mix_r, rs1_s, rs1_r, rs2_s, rs2_r, ini_ss, ini_r,
):
    rows = tokens.shape[0]
    cols = tokens.shape[1]
    chunks = rows // MB
    nb = n_seg * chunks
    half = nb // 2
    n_y = n_head // 2
    units = 2 * heads
    first = (n_seg - units) // 2
    sec = lax.axis_index("section")
    seg = lax.axis_index("seg")
    hd = lax.axis_index("head")
    y = hd // 2
    c = lax.rem(hd, 2)
    sib = 2 * y + 1 - c
    far = 1 - sec
    late = seg // (n_seg // 2)
    in_chain = jnp.logical_and(seg >= first, seg < first + units)
    unit = seg - first
    cg = unit // heads
    mine = unit - cg * heads
    holder = jnp.logical_and(in_chain, cg == c)

    def dev(s, h, x):
        return {"seg": s, "head": h, "section": x}

    def send(src, dst, s_sem, r_sem, device):
        return pltpu.make_async_remote_copy(
            src_ref=src, dst_ref=dst, send_sem=s_sem, recv_sem=r_sem,
            device_id=device, device_id_type=pl.DeviceIdType.MESH,
        )

    def span(ct):
        return pl.ds(pl.multiple_of(ct * MB, MB), MB)

    load_in = pltpu.make_async_copy(in_w.at[0], inw, wsem.at[0])
    load_out = pltpu.make_async_copy(out_w.at[0], outw, wsem.at[1])
    load_tok = pltpu.make_async_copy(tokens, hbuf.at[hd], tsem)

    @pl.when(sec == 0)
    def _():
        load_tok.start()

    load_in.start()
    load_out.start()

    barrier = pltpu.get_barrier_semaphore()

    def greet(device):
        pl.semaphore_signal(barrier, inc=1, device_id=device, device_id_type=pl.DeviceIdType.MESH)

    for k in range(1, n_head):
        greet(dev(seg, lax.rem(hd + k, n_head), sec))

    @pl.when(sec == 1)
    def _():
        greet(dev(seg, hd, 0))

    for j in range(heads):
        greet(dev(heads * c + j + first, 2 * y + 1 - late, far))

    @pl.when(in_chain)
    def _():
        for k in range(n_seg // 2):
            greet(dev(c * (n_seg // 2) + k, 2 * y + cg, far))
        greet(dev(seg, 2 * y + cg, far))

    total = n_head - 1 + heads + (1 - sec)
    total = total + jnp.where(in_chain, n_seg // 2, 0) + jnp.where(holder, 2, 0)
    pl.semaphore_wait(barrier, total)

    def direct(ct, k):
        to = jnp.int32(sib) if k == 0 else 2 * lax.rem(y + k, n_y) + c
        part = hbuf.at[hd, span(ct)]
        return send(part, part, ag_s.at[k, ct], ag_r.at[hd, ct], dev(seg, to, sec))

    def pass_on(ct, k):
        slot = 2 * lax.rem(y + k, n_y) + c
        part = hbuf.at[slot, span(ct)]
        return send(part, part, ag_s.at[n_y - 1 + k, ct], ag_r.at[slot, ct], dev(seg, sib, sec))

    def hop(ct):
        return send(panel.at[0, span(ct)], hbuf.at[hd, span(ct)], hop_s.at[ct], hop_r.at[ct], dev(seg, hd, 1))

    def arrived(slot, ct):
        part = hbuf.at[slot, span(ct)]
        send(part, part, ag_s.at[0, ct], ag_r.at[slot, ct], dev(seg, sib, sec)).wait_recv()

    flip = lax.rem(late + sec, 2)

    def need_order(t):
        return t + flip * (chunks - 1 - 2 * t)

    def done_order(t):
        return t + (1 - late) * (chunks - 1 - 2 * t)

    @pl.when(sec == 0)
    def _():
        load_tok.wait()

        def go(t, _):
            for k in (1, 3, 2, 0):
                direct(need_order(t), k).start()
            return 0

        lax.fori_loop(0, chunks, go, 0)

    def init_send(way):
        return send(ini_s.at[way], ini, ini_ss.at[way], ini_r, dev(seg, 2 * y + way, far))

    @pl.when(holder)
    def _():
        loads = []
        for way in range(2):
            loads.append(pltpu.make_async_copy(expand.at[0, way, mine], ini_s.at[way, pl.ds(0, 64)], isem.at[way]))
            loads.append(pltpu.make_async_copy(contract.at[0, way, mine], craw.at[way], isem.at[2 + way]))
        for copy in loads:
            copy.start()
        for copy in loads:
            copy.wait()
        every = rate[0]
        at_way = lax.broadcasted_iota(jnp.int32, every.shape, 0)
        at_head = lax.broadcasted_iota(jnp.int32, every.shape, 1)
        for way in range(2):
            ini_s[way, 64:128] = jnp.swapaxes(craw[way], 0, 1)
            picked = jnp.where((at_way == way) & (at_head == mine), every, 0.0)
            one = jnp.sum(picked, axis=(0, 1), keepdims=True) * (1.0 / (64 * MB))
            ini_s[way, 128:136] = jnp.broadcast_to(one, (8, 128))
            init_send(way).start()

    def push(ct, j):
        return send(
            stg.at[ct, j], xl.at[seg * chunks + ct], push_s.at[j, ct], ch_r.at[seg * chunks + ct],
            dev(heads * c + j + first, 2 * y + late, far),
        )

    lo = lax.broadcasted_iota(jnp.int32, (MB, 128), 1) < 64
    lo_half = lax.broadcasted_iota(jnp.int32, (MB // 2, 128), 1) < 64

    def project_role():
        load_in.wait()
        row = lax.broadcasted_iota(jnp.int32, (MB, 128), 0)
        io0 = lax.broadcasted_iota(jnp.int32, (128, 128), 0) // 64
        io1 = lax.broadcasted_iota(jnp.int32, (128, 128), 1) // 64
        ones = jnp.where(io0 == io1, 1.0 / 64, 0.0).astype(bf)

        def unit_rows(x):
            x = x.astype(bf).astype(f32)
            sq = x * x
            top = sq.astype(bf)
            low = (sq - top.astype(f32)).astype(bf)
            return x * lax.rsqrt(dot(top, ones) + dot(low, ones) + 1e-06)

        def one(t, _):
            ct = need_order(t)

            @pl.when(sec == 1)
            def _():
                hop(ct).wait_recv()
                for k in (1, 3, 2, 0):
                    direct(ct, k).start()

            for k in (1, 3, 2):
                arrived(2 * lax.rem(y + k, n_y) + c, ct)
                pass_on(ct, k).start()
            for k in (0, 1, 3, 2):
                arrived(2 * lax.rem(y + k, n_y) + 1 - c, ct)
            h = jnp.concatenate([hbuf[i, span(ct)] for i in range(n_head)], axis=1)
            proj = [dot(h, inw[i]) for i in range(3)]
            live = row + ct * MB < counts[0]
            for pair in range(heads // 2):
                at = slice(pair * 128, pair * 128 + 128)
                q = unit_rows(proj[0][:, at])
                k = unit_rows(proj[1][:, at])
                v = unit_rows(proj[2][:, at])
                d = jnp.where(live, k - v, 0.0)
                k = jnp.where(live, k, 0.0)
                top, bot = d[0 : MB // 2], d[MB // 2 :]
                stg[ct, 2 * pair, 0:64] = jnp.where(lo, q, pltpu.roll(k, 64, 1)).astype(bf)
                stg[ct, 2 * pair, 64:96] = jnp.where(lo_half, top, pltpu.roll(bot, 64, 1)).astype(bf)
                stg[ct, 2 * pair + 1, 0:64] = jnp.where(lo, pltpu.roll(q, 64, 1), k).astype(bf)
                stg[ct, 2 * pair + 1, 64:96] = jnp.where(lo_half, pltpu.roll(top, 64, 1), bot).astype(bf)
                push(ct, 2 * pair).start()
                push(ct, 2 * pair + 1).start()
            return 0

        lax.fori_loop(0, chunks, one, 0)

    def to_sibling(ct):
        return send(p1.at[ct], rs1.at[ct], rs1_s.at[ct], rs1_r.at[ct], dev(seg, sib, sec))

    def to_chip(ct, k):
        other = lax.rem(y + k, n_y)
        return send(p2.at[ct, k], rs2.at[ct, k], rs2_s.at[k, ct], rs2_r.at[k, ct], dev(seg, 2 * other + c, sec))

    def mix_in(ct, j):
        part = mixb.at[j, span(ct)]
        return send(part, part, mix_s.at[0], mix_r.at[j, ct], dev(seg, sib, sec))

    def columns(head):
        return pl.ds(pl.multiple_of(head * cols, 128), cols)

    def combine_role():
        load_out.wait()

        def multiply(ct):
            for j in range(heads):
                mix_in(ct, j).wait_recv()
            pairs = [mixb[2 * i, span(ct)] + mixb[2 * i + 1, span(ct)] for i in range(heads // 2)]
            mixture = jnp.concatenate(pairs, axis=1)
            for k in range(n_y):
                other = lax.rem(y + k, n_y)
                p1[ct, k] = dot(mixture, outw[:, columns(2 * other + 1 - c)]).astype(bf)
            to_sibling(ct).start()
            for k in range(n_y):
                other = lax.rem(y + k, n_y)
                p2f[ct, k] = dot(mixture, outw[:, columns(2 * other + c)])

        def reduce(ct):
            to_sibling(ct).wait_recv()
            for k in (1, 3, 2):
                p2[ct, k] = (p2f[ct, k] + rs1[ct, k].astype(f32)).astype(bf)
                to_chip(ct, k).start()

        def finish(t, _):
            ct = done_order(t)
            acc = p2f[ct, 0] + rs1[ct, 0].astype(f32)
            for k in (1, 3, 2):
                to_chip(ct, k).wait_recv()
                acc = acc + rs2[ct, k].astype(f32)
            panel[0, span(ct)] = (hbuf[hd, span(ct)].astype(f32) + acc).astype(bf)

            @pl.when(sec == 0)
            def _():
                hop(ct).start()

            return 0

        def two(t, _):
            @pl.when(t < chunks)
            def _():
                multiply(done_order(t))

            @pl.when(t > 0)
            def _():
                reduce(done_order(t - 1))

            return 0

        lax.fori_loop(0, chunks + 1, two, 0)
        lax.fori_loop(0, chunks, finish, 0)

    def at(i):
        return i + c * (nb - 1 - 2 * i)

    def landed(b):
        send(xl.at[b], xl.at[b], fw_s.at[0], ch_r.at[b], dev(seg, sib, sec)).wait_recv()

    def forward(i):
        b = at(i)
        return send(xl.at[b], xl.at[b], fw_s.at[i], ch_r.at[b], dev(seg, sib, sec))

    def exchange(i):
        return send(exs.at[i], exl.at[i], ex_s.at[i], ex_r.at[i], dev(seg, sib, sec))

    def give_back(i):
        b = at(i)
        return send(
            mxs.at[i - half], mixb.at[mine, span(lax.rem(b, chunks))], mix_s.at[i - half],
            mix_r.at[mine, lax.rem(b, chunks)], dev(b // chunks, 2 * y + cg, far),
        )

    def chain_role():
        init_send(0).wait_recv()
        u[...] = ini[0:64]
        w[...] = ini[64:128]
        sc = ini[128:129]
        ub[...] = jnp.zeros_like(ub)
        wk[...] = jnp.zeros_like(wk)
        ub[64:128] = ini[0:64].astype(bf)
        wk[64:128] = ini[64:128].astype(bf)
        landed(at(0))
        forward(0).start()
        z = dot(xl[at(0), 0:64], ub[0:128])

        def mixed(i, out):
            exchange(nb - 1 - i).wait_recv()
            both = jnp.where(lo, 0.0, out + exl[nb - 1 - i])
            both = jnp.where(lax.rem(mine, 2) == 0, pltpu.roll(both, 64, 1), both)
            mxs[i - half] = both.astype(bf)
            give_back(i).start()

        def early(i, carry):
            landed(at(i + 1))

            @pl.when(i + 1 < half)
            def _():
                forward(i + 1).start()

            before = jnp.maximum(i - 1, 0)
            zn, back, out = chain_step(xl, at(before), at(i), at(i + 1), carry[0], carry[1], sc, u, w, ub, wk)
            exs[before] = out

            @pl.when(i > 0)
            def _():
                exchange(before).start()

            return zn, back

        def later(i, carry):
            after = jnp.minimum(i + 1, nb - 1)

            @pl.when(i + 1 < nb)
            def _():
                landed(at(after))

            zn, back, out = chain_step(xl, at(i - 1), at(i), at(after), carry[0], carry[1], sc, u, w, ub, wk)
            mixed(i - 1, out)
            return zn, back

        carry = lax.fori_loop(0, half + 1, early, (z, jnp.zeros((64, 128), bf)))
        carry = lax.fori_loop(half + 1, nb, later, carry)
        last = xl[at(nb - 1), 0:64]
        ub[64:128] = (u[...] - dot_tn(last, carry[1])[64:128]).astype(bf)
        aq = smooth(dot(last, ub[64:192])).astype(bf)
        mixed(nb - 1, pltpu.roll(last.astype(f32), 64, 1) + dot_nt(aq, wk[...]))

        def drain(i, _):
            forward(i).wait_send()
            exchange(i).wait_send()
            give_back(half + i).wait_send()
            return 0

        lax.fori_loop(0, half, drain, 0)

    def turn(t, _):
        @pl.when(jnp.logical_and(in_chain, sec + t == 1))
        def _():
            chain_role()

        @pl.when(t == 0)
        def _():
            project_role()
            combine_role()

        return 0

    lax.fori_loop(0, 2, turn, 0)

    def drain(ct, _):
        for k in range(n_y):
            direct(ct, k).wait_send()
        for k in range(1, n_y):
            pass_on(ct, k).wait_send()
            to_chip(ct, k).wait_send()
        for j in range(heads):
            push(ct, j).wait_send()
        to_sibling(ct).wait_send()

        @pl.when(sec == 0)
        def _():
            hop(ct).wait_send()

        return 0

    lax.fori_loop(0, chunks, drain, 0)

    @pl.when(holder)
    def _():
        init_send(0).wait_send()
        init_send(1).wait_send()


def solution(mesh):
    n_seg, n_head = mesh.shape["seg"], mesh.shape["head"]
    placed = (
        P("seg", "head"),
        P("section", None, None, "head"),
        P("section", "head", None),
        P("section", None, "head", None, None),
        P("section", None, "head", None, None),
        P("section", None, "head"),
        P("seg"),
    )

    def local(tokens, in_weight, out_weight, expand_init, contract_init, inner_rate, seg_counts):
        rows, cols = tokens.shape
        heads = expand_init.shape[2]
        chunks = rows // MB
        nb = n_seg * chunks
        n_y = n_head // 2
        any_space = pl.BlockSpec(memory_space=pl.ANY)
        vmem = pl.BlockSpec(memory_space=pltpu.VMEM)
        smem = pl.BlockSpec(memory_space=pltpu.SMEM)
        dma = pltpu.SemaphoreType.DMA
        return pl.pallas_call(
            functools.partial(kernel, n_seg, n_head, heads),
            out_shape=jax.ShapeDtypeStruct((1, rows, cols), bf),
            in_specs=[any_space] * 5 + [vmem, smem],
            out_specs=vmem,
            scratch_shapes=[
                pltpu.VMEM(in_weight.shape[1:], bf),
                pltpu.VMEM(out_weight.shape[1:], bf),
                pltpu.VMEM((n_head, rows, cols), bf),
                pltpu.VMEM((chunks, heads, 96, 128), bf),
                pltpu.VMEM((nb, 96, 128), bf),
                pltpu.VMEM((2, 136, 128), f32),
                pltpu.VMEM((136, 128), f32),
                pltpu.VMEM((2, 128, 64), f32),
                pltpu.VMEM((nb // 2, 64, 128), f32),
                pltpu.VMEM((nb // 2, 64, 128), f32),
                pltpu.VMEM((nb // 2, 64, 128), bf),
                pltpu.VMEM((heads, rows, 128), bf),
                pltpu.VMEM((chunks, n_y, MB, cols), bf),
                pltpu.VMEM((chunks, n_y, MB, cols), f32),
                pltpu.VMEM((chunks, n_y, MB, cols), bf),
                pltpu.VMEM((chunks, n_y, MB, cols), bf),
                pltpu.VMEM((chunks, n_y, MB, cols), bf),
                pltpu.VMEM((64, 128), f32),
                pltpu.VMEM((64, 128), f32),
                pltpu.VMEM((192, 128), bf),
                pltpu.VMEM((128, 128), bf),
                dma((2,)),
                dma,
                dma((4,)),
                dma((2 * n_y - 1, chunks)),
                dma((n_head, chunks)),
                dma((chunks,)),
                dma((chunks,)),
                dma((heads, chunks)),
                dma((nb,)),
                dma((nb // 2,)),
                dma((nb // 2,)),
                dma((nb // 2,)),
                dma((nb // 2,)),
                dma((heads, chunks)),
                dma((chunks,)),
                dma((chunks,)),
                dma((n_y, chunks)),
                dma((n_y, chunks)),
                dma((2,)),
                dma,
            ],
            compiler_params=pltpu.CompilerParams(
                collective_id=0, has_side_effects=True, vmem_limit_bytes=44 << 20
            ),
            name="both_groups",
        )(tokens, in_weight, out_weight, expand_init, contract_init, inner_rate, seg_counts)

    return jax.shard_map(
        local, mesh=mesh, in_specs=placed, out_specs=P("section", "seg", "head"), check_vma=False
    )
```

```python
import functools
import math

import jax
import jax.numpy as jnp
from jax import lax
from jax.experimental import pallas as pl
from jax.experimental.pallas import tpu as pltpu
from jax.sharding import PartitionSpec as P

MB = 64
C1 = math.sqrt(2.0 / math.pi)
C3 = 0.044715
f32 = jnp.float32
bf = jnp.bfloat16


def dot(a, b):
    return lax.dot_general(a, b, (((1,), (0,)), ((), ())), preferred_element_type=f32)


def dot_nt(a, b):
    return lax.dot_general(a, b, (((1,), (1,)), ((), ())), preferred_element_type=f32)


def dot_tn(a, b):
    return lax.dot_general(a, b, (((0,), (0,)), ((), ())), preferred_element_type=f32)


def smooth(z):
    t = jnp.tanh(z * (C1 + (C1 * C3) * (z * z)))
    h = 0.5 * z
    return h + h * t


def smooth_slope(z):
    z2 = z * z
    t = jnp.tanh(z * (C1 + (C1 * C3) * z2))
    h = 0.5 * z
    return h + h * t, 0.5 + 0.5 * t + h * (1.0 - t * t) * (C1 + (3.0 * C1 * C3) * z2)


def chain_step(xl, bp, b, bn, z, bk, sc, u, w, ub, wk):
    xp, xb, xn = xl[bp, 0:64], xl[b, 0:64], xl[bn, 0:64]
    dp = xl[b, 64:96].astype(f32)
    hi = lax.broadcasted_iota(jnp.int32, (64, 128), 1) >= 64
    a, s = smooth_slope(z)
    s = s * sc
    ab = a.astype(bf)
    wkv = wk[...]
    delta = jnp.where(hi, jnp.concatenate([pltpu.roll(dp, 64, 1), dp], 0), 0.0)
    e = delta + dot(ab, wkv)
    back = (dot_nt(e.astype(bf), wkv) * s).astype(bf)
    un = u[...] - dot_tn(xp, bk)[64:128]
    u[...] = un
    ub[64:128] = un.astype(bf)
    zq = dot(xp, ub[64:192])
    gram = dot_nt(jnp.where(hi, xn, jnp.zeros_like(xn)), xb).astype(bf)
    zn = dot(xn, ub[0:128]) - dot(gram, back)
    aq = smooth(zq).astype(bf)
    out = pltpu.roll(xp.astype(f32), 64, 1) + dot(aq, wkv)
    wn = w[...] - dot_tn(ab, (e * sc).astype(bf))
    w[...] = wn
    wk[...] = wn.astype(bf)
    return zn, back, out


def kernel(
    n_seg, n_head, heads,
    tokens, in_w, out_w, expand, contract, rate, counts,
    panel,
    inw, outw, hbuf, stg, xl, ini_s, ini, exs, exl, mxs, mixb,
    p1, p2f, rs1, p2, rs2, u, w, ub, wk,
    wsem, tsem, isem, ag_s, ag_r, po_s, hop_s, push_s, ch_r, fw_s, fw_r, ex_s, ex_r,
    mix_s, mix_r, rs1_s, rs1_r, rs2_s, rs2_r, ini_ss, ini_r,
):
    rows = tokens.shape[0]
    cols = tokens.shape[1]
    chunks = rows // MB
    nb = n_seg * chunks
    half = nb // 2
    n_y = n_head // 2
    line = n_seg // 2
    turn_by = line // 2 + 1
    sec = lax.axis_index("section")
    seg = lax.axis_index("seg")
    hd = lax.axis_index("head")
    y = hd // 2
    c = lax.rem(hd, 2)
    sib = 2 * y + 1 - c
    far = 1 - sec
    late = seg // line
    spot = lax.rem(lax.rem(seg, line) + line - turn_by, line)
    in_chain = spot < heads
    cg = late
    mine = jnp.minimum(spot, heads - 1)
    edge = jnp.logical_or(seg < 2, seg >= n_seg - 2)

    def place(group, j):
        return group * line + lax.rem(j + turn_by, line)

    holder = jnp.logical_and(in_chain, cg == c)

    def dev(s, h, x):
        return {"seg": s, "head": h, "section": x}

    def send(src, dst, s_sem, r_sem, device):
        return pltpu.make_async_remote_copy(
            src_ref=src, dst_ref=dst, send_sem=s_sem, recv_sem=r_sem,
            device_id=device, device_id_type=pl.DeviceIdType.MESH,
        )

    def span(ct):
        return pl.ds(pl.multiple_of(ct * MB, MB), MB)

    load_in = pltpu.make_async_copy(in_w.at[0], inw, wsem.at[0])
    load_out = pltpu.make_async_copy(out_w.at[0], outw, wsem.at[1])
    load_tok = pltpu.make_async_copy(tokens, hbuf.at[hd], tsem)

    @pl.when(sec == 0)
    def _():
        load_tok.start()

    load_in.start()
    load_out.start()

    barrier = pltpu.get_barrier_semaphore()

    def greet(device):
        pl.semaphore_signal(barrier, inc=1, device_id=device, device_id_type=pl.DeviceIdType.MESH)

    for j in range(heads):
        greet(dev(place(c, j), 2 * y + 1 - late, far))

    @pl.when(in_chain)
    def _():
        for k in range(line):
            greet(dev(c * line + k, 2 * y + cg, far))
        greet(dev(seg, 2 * y + cg, far))

    @pl.when(sec == 1)
    def _():
        for k in range(n_y):
            greet(dev(seg, 2 * k + c, 0))

    for k in range(1, n_head):
        greet(dev(seg, lax.rem(hd + k, n_head), sec))

    @pl.when(holder)
    def _():
        loads = []
        for way in range(2):
            loads.append(pltpu.make_async_copy(expand.at[0, way, mine], ini_s.at[way, pl.ds(0, 64)], isem.at[way]))
            loads.append(
                pltpu.make_async_copy(contract.at[0, way, mine], ini_s.at[way, pl.ds(64, 64)], isem.at[2 + way])
            )
        for copy in loads:
            copy.start()
        every = rate[0]
        at_way = lax.broadcasted_iota(jnp.int32, every.shape, 0)
        at_head = lax.broadcasted_iota(jnp.int32, every.shape, 1)
        for way in range(2):
            picked = jnp.where((at_way == way) & (at_head == mine), every, 0.0)
            one = jnp.sum(picked, axis=(0, 1), keepdims=True) * (1.0 / (64 * MB))
            ini_s[way, 128:136] = jnp.broadcast_to(one, (8, 128))
        for copy in loads:
            copy.wait()

    @pl.when(sec == 0)
    def _():
        load_tok.wait()

    total = n_head - 1 + heads + n_y * (1 - sec)
    total = total + jnp.where(in_chain, line, 0) + jnp.where(holder, 2, 0)
    pl.semaphore_wait(barrier, total)

    def direct(ct, k):
        part = hbuf.at[hd, span(ct)]
        return send(part, part, ag_s.at[k, ct], ag_r.at[hd, ct], dev(seg, 2 * lax.rem(y + k, n_y) + c, sec))

    def hop(ct, k):
        return send(
            panel.at[0, span(ct)], hbuf.at[hd, span(ct)], hop_s.at[k, ct], ag_r.at[hd, ct],
            dev(seg, 2 * lax.rem(y + k, n_y) + c, 1),
        )

    def pass_on(ct, k):
        slot = 2 * lax.rem(y + k, n_y) + c
        part = hbuf.at[slot, span(ct)]
        return send(part, part, po_s.at[k, ct], ag_r.at[slot, ct], dev(seg, sib, sec))

    def arrived(slot, ct):
        part = hbuf.at[slot, span(ct)]
        send(part, part, po_s.at[0, ct], ag_r.at[slot, ct], dev(seg, sib, sec)).wait_recv()

    flip = lax.rem(late + sec, 2)

    def need_order(t):
        return t + flip * (chunks - 1 - 2 * t)

    def done_order(t):
        return t + (1 - late) * (chunks - 1 - 2 * t)

    @pl.when(sec == 0)
    def _():
        def go(t, _):
            for k in (2, 1, 3):
                direct(need_order(t), k).start()
            return 0

        lax.fori_loop(0, chunks, go, 0)

    def init_send(way):
        return send(ini_s.at[way], ini, ini_ss.at[way], ini_r, dev(seg, 2 * y + way, far))

    @pl.when(holder)
    def _():
        init_send(0).start()
        init_send(1).start()

    def push(ct, j):
        return send(
            stg.at[ct, j], xl.at[seg * chunks + ct], push_s.at[j, ct], ch_r.at[seg * chunks + ct],
            dev(place(c, j), 2 * y + late, far),
        )

    lo = lax.broadcasted_iota(jnp.int32, (MB, 128), 1) < 64
    lo_half = lax.broadcasted_iota(jnp.int32, (MB // 2, 128), 1) < 64

    def project_role():
        load_in.wait()
        row = lax.broadcasted_iota(jnp.int32, (MB, 128), 0)
        io0 = lax.broadcasted_iota(jnp.int32, (128, 128), 0) // 64
        io1 = lax.broadcasted_iota(jnp.int32, (128, 128), 1) // 64
        ones = jnp.where(io0 == io1, 1.0 / 64, 0.0).astype(bf)

        def unit_rows(x):
            x = x.astype(bf).astype(f32)
            sq = x * x
            top = sq.astype(bf)
            low = (sq - top.astype(f32)).astype(bf)
            return x * lax.rsqrt(dot(top, ones) + dot(low, ones) + 1e-06)

        def one(t, _):
            ct = need_order(t)

            @pl.when(sec == 1)
            def _():
                arrived(hd, ct)

            pass_on(ct, 0).start()
            for k in (1, 3, 2):
                arrived(2 * lax.rem(y + k, n_y) + c, ct)
                pass_on(ct, k).start()
            for k in (0, 1, 3, 2):
                arrived(2 * lax.rem(y + k, n_y) + 1 - c, ct)
            h = jnp.concatenate([hbuf[i, span(ct)] for i in range(n_head)], axis=1)
            proj = [dot(h, inw[i]) for i in range(3)]
            live = row + ct * MB < counts[0]
            for pair in range(heads // 2):
                at = slice(pair * 128, pair * 128 + 128)
                q = unit_rows(proj[0][:, at])
                k = unit_rows(proj[1][:, at])
                v = unit_rows(proj[2][:, at])
                d = jnp.where(live, k - v, 0.0)
                k = jnp.where(live, k, 0.0)
                top, bot = d[0 : MB // 2], d[MB // 2 :]
                stg[ct, 2 * pair, 0:64] = jnp.where(lo, q, pltpu.roll(k, 64, 1)).astype(bf)
                stg[ct, 2 * pair, 64:96] = jnp.where(lo_half, top, pltpu.roll(bot, 64, 1)).astype(bf)
                stg[ct, 2 * pair + 1, 0:64] = jnp.where(lo, pltpu.roll(q, 64, 1), k).astype(bf)
                stg[ct, 2 * pair + 1, 64:96] = jnp.where(lo_half, pltpu.roll(top, 64, 1), bot).astype(bf)

                @pl.when(edge)
                def _():
                    push(ct, 2 * pair).start()
                    push(ct, 2 * pair + 1).start()

            return 0

        lax.fori_loop(0, chunks, one, 0)

        @pl.when(jnp.logical_not(edge))
        def _():
            def rest(t, _):
                for j in range(heads):
                    push(need_order(t), j).start()
                return 0

            lax.fori_loop(0, chunks, rest, 0)

    def to_sibling(ct):
        return send(p1.at[ct], rs1.at[ct], rs1_s.at[ct], rs1_r.at[ct], dev(seg, sib, sec))

    def to_chip(ct, k):
        other = lax.rem(y + k, n_y)
        return send(p2.at[ct, k], rs2.at[ct, k], rs2_s.at[k, ct], rs2_r.at[k, ct], dev(seg, 2 * other + c, sec))

    def mix_in(ct, j):
        part = mixb.at[j, span(ct)]
        return send(part, part, mix_s.at[0], mix_r.at[j, ct], dev(seg, sib, sec))

    def columns(head):
        return pl.ds(pl.multiple_of(head * cols, 128), cols)

    def combine_role():
        load_out.wait()

        def multiply(ct):
            for j in range(heads):
                mix_in(ct, j).wait_recv()
            pairs = [mixb[2 * i, span(ct)] + mixb[2 * i + 1, span(ct)] for i in range(heads // 2)]
            mixture = jnp.concatenate(pairs, axis=1)
            for k in range(n_y):
                other = lax.rem(y + k, n_y)
                p1[ct, k] = dot(mixture, outw[:, columns(2 * other + 1 - c)]).astype(bf)
            to_sibling(ct).start()
            for k in range(n_y):
                other = lax.rem(y + k, n_y)
                p2f[ct, k] = dot(mixture, outw[:, columns(2 * other + c)])

        def reduce(ct):
            to_sibling(ct).wait_recv()
            for k in (1, 3, 2):
                p2[ct, k] = (p2f[ct, k] + rs1[ct, k].astype(f32)).astype(bf)
                to_chip(ct, k).start()

        def finish(t, _):
            ct = done_order(t)
            acc = p2f[ct, 0] + rs1[ct, 0].astype(f32)
            for k in (1, 3, 2):
                to_chip(ct, k).wait_recv()
                acc = acc + rs2[ct, k].astype(f32)
            panel[0, span(ct)] = (hbuf[hd, span(ct)].astype(f32) + acc).astype(bf)

            @pl.when(sec == 0)
            def _():
                for k in (2, 1, 3, 0):
                    hop(ct, k).start()

            return 0

        def two(t, _):
            @pl.when(t < chunks)
            def _():
                multiply(done_order(t))

            @pl.when(t > 0)
            def _():
                reduce(done_order(t - 1))

            return 0

        lax.fori_loop(0, chunks + 1, two, 0)
        lax.fori_loop(0, chunks, finish, 0)

    def at(i):
        return i + c * (nb - 1 - 2 * i)

    def landed(i):
        b = at(i)
        send(xl.at[b], xl.at[b], fw_s.at[0], ch_r.at[b], dev(seg, sib, sec)).wait_recv()

    def three(g):
        return xl.at[pl.ds((g + c * (n_seg - 1 - 2 * g)) * chunks, chunks)]

    def forward(g):
        return send(three(g), three(g), fw_s.at[g], fw_r.at[g], dev(seg, sib, sec))

    def other_half(g):
        back = n_seg - 1 - g
        send(three(g), three(g), fw_s.at[back], fw_r.at[back], dev(seg, sib, sec)).wait_recv()

    def exchange(g):
        return send(exs.at[g], exl.at[g], ex_s.at[g], ex_r.at[g], dev(seg, sib, sec))

    def give_back(i):
        b = at(i)
        return send(
            mxs.at[i - half], mixb.at[mine, span(lax.rem(b, chunks))], mix_s.at[i - half],
            mix_r.at[mine, lax.rem(b, chunks)], dev(b // chunks, 2 * y + cg, far),
        )

    def chain_role():
        ub[...] = jnp.zeros_like(ub)
        init_send(0).wait_recv()
        u[...] = ini[0:64]
        ub[64:128] = ini[0:64].astype(bf)
        w0 = jnp.concatenate([jnp.zeros((128, 64), f32), jnp.swapaxes(ini[64:128], 0, 1)], axis=1)
        w[...] = w0
        wk[...] = w0.astype(bf)
        sc = ini[128:129]
        landed(0)
        z = dot(xl[at(0), 0:64], ub[0:128])

        def mixed(m, t, mine_out):
            i = chunks * m + t - 1
            slot = nb + 1 - chunks * m - t
            both = mine_out + exl[slot // chunks, lax.rem(slot, chunks)]
            both = jnp.where(lo, 0.0, both)
            both = jnp.where(lax.rem(mine, 2) == 0, pltpu.roll(both, 64, 1), both)
            mxs[i - half] = both.astype(bf)
            give_back(i).start()

        def group(g, carry):
            @pl.when(g == 0)
            def _():
                for i in range(1, chunks + 1):
                    landed(i)
                forward(0).start()

            @pl.when(g == 1)
            def _():
                for i in range(chunks + 1, 2 * chunks):
                    landed(i)
                forward(1).start()

            @pl.when(jnp.logical_and(g >= 1, g < line - 1))
            def _():
                for i in range(chunks):
                    landed(chunks * (g + 1) + i)
                forward(g + 1).start()

            @pl.when(jnp.logical_and(g >= line - 1, g < n_seg - 1))
            def _():
                other_half(g + 1)

            z, back = carry
            for t in range(chunks):
                i = chunks * g + t
                before, after = jnp.maximum(i - 1, 0), jnp.minimum(i + 1, nb - 1)
                z, back, out = chain_step(xl, at(before), at(i), at(after), z, back, sc, u, w, ub, wk)
                exs[g, t] = out

            @pl.when(g <= line)
            def _():
                exchange(g).start()

            @pl.when(g > line)
            def _():
                m = g - 1

                @pl.when(m == line)
                def _():
                    exchange(line).wait_recv()

                exchange(n_seg - 1 - m).wait_recv()

                @pl.when(m > line)
                def _():
                    mixed(m, 0, exs[m, 0])

                for t in range(1, chunks):
                    mixed(m, t, exs[m, t])

            return z, back

        carry = lax.fori_loop(0, n_seg, group, (z, jnp.zeros((64, 128), bf)))
        exchange(0).wait_recv()
        for t in range(chunks):
            mixed(n_seg - 1, t, exs[n_seg - 1, t])
        last = xl[at(nb - 1), 0:64]
        ub[64:128] = (u[...] - dot_tn(last, carry[1])[64:128]).astype(bf)
        aq = smooth(dot(last, ub[64:192])).astype(bf)
        mixed(n_seg, 0, pltpu.roll(last.astype(f32), 64, 1) + dot(aq, wk[...]))

        def drain(i, _):
            give_back(half + i).wait_send()
            return 0

        lax.fori_loop(0, half, drain, 0)
        for g in range(line):
            forward(g).wait_send()
        for g in range(line + 1):
            exchange(g).wait_send()

    def turn(t, _):
        @pl.when(jnp.logical_and(in_chain, sec + t == 1))
        def _():
            chain_role()

        @pl.when(t == 0)
        def _():
            project_role()
            combine_role()

        return 0

    lax.fori_loop(0, 2, turn, 0)

    def drain(ct, _):
        for k in range(n_y):
            pass_on(ct, k).wait_send()
        for k in range(1, n_y):
            to_chip(ct, k).wait_send()
        for j in range(heads):
            push(ct, j).wait_send()
        to_sibling(ct).wait_send()

        @pl.when(sec == 0)
        def _():
            for k in range(n_y):
                hop(ct, k).wait_send()
            for k in range(1, n_y):
                direct(ct, k).wait_send()

        return 0

    lax.fori_loop(0, chunks, drain, 0)

    @pl.when(holder)
    def _():
        init_send(0).wait_send()
        init_send(1).wait_send()


def solution(mesh):
    n_seg, n_head = mesh.shape["seg"], mesh.shape["head"]
    placed = (
        P("seg", "head"),
        P("section", None, None, "head"),
        P("section", "head", None),
        P("section", None, "head", None, None),
        P("section", None, "head", None, None),
        P("section", None, "head"),
        P("seg"),
    )

    def local(tokens, in_weight, out_weight, expand_init, contract_init, inner_rate, seg_counts):
        rows, cols = tokens.shape
        heads = expand_init.shape[2]
        chunks = rows // MB
        nb = n_seg * chunks
        n_y = n_head // 2
        any_space = pl.BlockSpec(memory_space=pltpu.HBM)
        vmem = pl.BlockSpec(memory_space=pltpu.VMEM)
        smem = pl.BlockSpec(memory_space=pltpu.SMEM)
        dma = pltpu.SemaphoreType.DMA
        return pl.pallas_call(
            functools.partial(kernel, n_seg, n_head, heads),
            out_shape=jax.ShapeDtypeStruct((1, rows, cols), bf),
            in_specs=[any_space] * 5 + [vmem, smem],
            out_specs=vmem,
            scratch_shapes=[
                pltpu.VMEM(in_weight.shape[1:], bf),
                pltpu.VMEM(out_weight.shape[1:], bf),
                pltpu.VMEM((n_head, rows, cols), bf),
                pltpu.VMEM((chunks, heads, 96, 128), bf),
                pltpu.VMEM((nb, 96, 128), bf),
                pltpu.VMEM((2, 136, 128), f32),
                pltpu.VMEM((136, 128), f32),
                pltpu.VMEM((n_seg, chunks, 64, 128), f32),
                pltpu.VMEM((n_seg // 2 + 1, chunks, 64, 128), f32),
                pltpu.VMEM((nb // 2, 64, 128), bf),
                pltpu.VMEM((heads, rows, 128), bf),
                pltpu.VMEM((chunks, n_y, MB, cols), bf),
                pltpu.VMEM((chunks, n_y, MB, cols), f32),
                pltpu.VMEM((chunks, n_y, MB, cols), bf),
                pltpu.VMEM((chunks, n_y, MB, cols), bf),
                pltpu.VMEM((chunks, n_y, MB, cols), bf),
                pltpu.VMEM((64, 128), f32),
                pltpu.VMEM((128, 128), f32),
                pltpu.VMEM((192, 128), bf),
                pltpu.VMEM((128, 128), bf),
                dma((2,)),
                dma,
                dma((4,)),
                dma((n_y, chunks)),
                dma((n_head, chunks)),
                dma((n_y, chunks)),
                dma((n_y, chunks)),
                dma((heads, chunks)),
                dma((nb,)),
                dma((n_seg // 2,)),
                dma((n_seg // 2,)),
                dma((n_seg // 2 + 1,)),
                dma((n_seg // 2 + 1,)),
                dma((nb // 2,)),
                dma((heads, chunks)),
                dma((chunks,)),
                dma((chunks,)),
                dma((n_y, chunks)),
                dma((n_y, chunks)),
                dma((2,)),
                dma,
            ],
            compiler_params=pltpu.CompilerParams(
                collective_id=0, has_side_effects=True, vmem_limit_bytes=60 << 20
            ),
            name="both_groups",
        )(tokens, in_weight, out_weight, expand_init, jnp.swapaxes(contract_init, 3, 4), inner_rate, seg_counts)

    return jax.shard_map(
        local, mesh=mesh, in_specs=placed, out_specs=P("section", "seg", "head"), check_vma=False
    )
```

```python
import functools
import math

import jax
import jax.numpy as jnp
from jax import lax
from jax.experimental import pallas as pl
from jax.experimental.pallas import tpu as pltpu
from jax.sharding import PartitionSpec as P

MB = 64
C1 = math.sqrt(2.0 / math.pi)
C3 = 0.044715
f32 = jnp.float32
bf = jnp.bfloat16


def dot(a, b):
    return lax.dot_general(a, b, (((1,), (0,)), ((), ())), preferred_element_type=f32)


def dot_nt(a, b):
    return lax.dot_general(a, b, (((1,), (1,)), ((), ())), preferred_element_type=f32)


def dot_tn(a, b):
    return lax.dot_general(a, b, (((0,), (0,)), ((), ())), preferred_element_type=f32)


def smooth(z):
    t = jnp.tanh(z * (C1 + (C1 * C3) * (z * z)))
    h = 0.5 * z
    return h + h * t


def smooth_slope(z):
    z2 = z * z
    t = jnp.tanh(z * (C1 + (C1 * C3) * z2))
    h = 0.5 * z
    return h + h * t, 0.5 + 0.5 * t + h * (1.0 - t * t) * (C1 + (3.0 * C1 * C3) * z2)


def chain_step(xl, bp, b, bn, z, bk, sc, u, w, ub, wk):
    xp, xb, xn = xl[bp, 0:64], xl[b, 0:64], xl[bn, 0:64]
    dp = xl[b, 64:96].astype(f32)
    hi = lax.broadcasted_iota(jnp.int32, (64, 128), 1) >= 64
    a, s = smooth_slope(z)
    s = s * sc
    ab = a.astype(bf)
    wkv = wk[...]
    delta = jnp.where(hi, jnp.concatenate([pltpu.roll(dp, 64, 1), dp], 0), 0.0)
    e = delta + dot(ab, wkv)
    back = (dot_nt(e.astype(bf), wkv) * s).astype(bf)
    un = u[...] - dot_tn(xp, bk)[64:128]
    u[...] = un
    ub[64:128] = un.astype(bf)
    zq = dot(xp, ub[64:192])
    gram = dot_nt(jnp.where(hi, xn, jnp.zeros_like(xn)), xb).astype(bf)
    zn = dot(xn, ub[0:128]) - dot(gram, back)
    aq = smooth(zq).astype(bf)
    out = pltpu.roll(xp.astype(f32), 64, 1) + dot(aq, wkv)
    wn = w[...] - dot_tn(ab, (e * sc).astype(bf))
    w[...] = wn
    wk[...] = wn.astype(bf)
    return zn, back, out


def kernel(
    n_seg, n_head, heads,
    tokens, in_w, out_w, expand, contract, rate, counts,
    panel,
    inw, outw, hbuf, acc, stg, xl, ini_s, ini, exs, exl, mxs, mixb,
    p1, p2f, rs1, p2, rs2, u, w, ub, wk,
    wsem, tsem, isem, ag_s, ag_r, po_s, hop_s, push_s, ch_r, fw_s, ex_s, ex_r,
    mix_s, mix_r, rs1_s, rs1_r, rs2_s, rs2_r, ini_ss, ini_r,
):
    rows = tokens.shape[0]
    cols = tokens.shape[1]
    chunks = rows // MB
    nb = n_seg * chunks
    half = nb // 2
    n_y = n_head // 2
    line = n_seg // 2
    turn_by = line // 2 + 1
    sec = lax.axis_index("section")
    seg = lax.axis_index("seg")
    hd = lax.axis_index("head")
    y = hd // 2
    c = lax.rem(hd, 2)
    sib = 2 * y + 1 - c
    late = seg // line
    spot = lax.rem(lax.rem(seg, line) + line - turn_by, line)
    in_chain = spot < heads
    cg = late
    mine = jnp.minimum(spot, heads - 1)

    def place(group, j):
        return group * line + lax.rem(j + turn_by, line)

    holder = jnp.logical_and(in_chain, cg == c)

    def dev(s, h, x):
        return {"seg": s, "head": h, "section": x}

    def send(src, dst, s_sem, r_sem, device):
        return pltpu.make_async_remote_copy(
            src_ref=src, dst_ref=dst, send_sem=s_sem, recv_sem=r_sem,
            device_id=device, device_id_type=pl.DeviceIdType.MESH,
        )

    def span(ct):
        return pl.ds(pl.multiple_of(ct * MB, MB), MB)

    load_in = pltpu.make_async_copy(in_w.at[0], inw, wsem.at[0])
    load_out = pltpu.make_async_copy(out_w.at[0], outw, wsem.at[1])
    load_tok = pltpu.make_async_copy(tokens, hbuf.at[hd], tsem)

    @pl.when(sec == 0)
    def _():
        load_tok.start()

    load_in.start()
    load_out.start()

    barrier = pltpu.get_barrier_semaphore()

    def greet(device):
        pl.semaphore_signal(barrier, inc=1, device_id=device, device_id_type=pl.DeviceIdType.MESH)

    for j in range(heads):
        greet(dev(place(c, j), 2 * y + 1 - late, sec))

    @pl.when(in_chain)
    def _():
        for k in range(line):
            source = c * line + k

            @pl.when(jnp.logical_not(jnp.logical_and(holder, source == seg)))
            def _():
                greet(dev(source, 2 * y + cg, sec))

    @pl.when(sec == 1)
    def _():
        greet(dev(seg, hd, 0))

    for k in range(1, n_head):
        greet(dev(seg, lax.rem(hd + k, n_head), sec))

    @pl.when(holder)
    def _():
        loads = []
        for way, to in ((c, ini), (1 - c, ini_s)):
            loads.append(pltpu.make_async_copy(expand.at[0, way, mine], to.at[pl.ds(0, 64)], isem.at[len(loads)]))
            loads.append(pltpu.make_async_copy(contract.at[0, way, mine], to.at[pl.ds(64, 64)], isem.at[len(loads)]))
        for copy in loads:
            copy.start()
        every = rate[0]
        at_way = lax.broadcasted_iota(jnp.int32, every.shape, 0)
        at_head = lax.broadcasted_iota(jnp.int32, every.shape, 1)
        for way, to in ((c, ini), (1 - c, ini_s)):
            picked = jnp.where((at_way == way) & (at_head == mine), every, 0.0)
            one = jnp.sum(picked, axis=(0, 1), keepdims=True) * (1.0 / (64 * MB))
            to[128:136] = jnp.broadcast_to(one, (8, 128))
        for copy in loads:
            copy.wait()

    @pl.when(sec == 0)
    def _():
        load_tok.wait()

    total = n_head - 1 + heads + (1 - sec)
    total = total + jnp.where(in_chain, line, 0) - jnp.where(holder, 1, 0)
    pl.semaphore_wait(barrier, total)

    def direct(ct, k):
        part = hbuf.at[hd, span(ct)]
        return send(part, part, ag_s.at[k, ct], ag_r.at[hd, ct], dev(seg, 2 * lax.rem(y + k, n_y) + c, sec))

    def hop(ct):
        return send(panel.at[0, span(ct)], hbuf.at[hd, span(ct)], hop_s.at[ct], ag_r.at[hd, ct], dev(seg, hd, 1))

    def pass_on(ct, k):
        slot = 2 * lax.rem(y + k, n_y) + c
        part = hbuf.at[slot, span(ct)]
        return send(part, part, po_s.at[k, ct], ag_r.at[slot, ct], dev(seg, sib, sec))

    def arrived(slot, ct):
        part = hbuf.at[slot, span(ct)]
        send(part, part, po_s.at[0, ct], ag_r.at[slot, ct], dev(seg, sib, sec)).wait_recv()

    flip = lax.rem(late + sec, 2)

    def need_order(t):
        return t + flip * (chunks - 1 - 2 * t)

    def done_order(t):
        return t + (1 - late) * (chunks - 1 - 2 * t)

    @pl.when(sec == 0)
    def _():
        def go(t, _):
            for k in (2, 1, 3):
                direct(need_order(t), k).start()
            return 0

        lax.fori_loop(0, chunks, go, 0)

    init_send = send(ini_s, ini, ini_ss, ini_r, dev(seg, sib, sec))

    @pl.when(holder)
    def _():
        init_send.start()

    def push(j):
        return send(
            stg.at[j], xl.at[pl.ds(seg * chunks, chunks)], push_s.at[j], ch_r.at[seg],
            dev(place(c, j), 2 * y + late, sec),
        )

    def give(j):
        own = jnp.logical_and(holder, mine == j)

        @pl.when(own)
        def _():
            pltpu.make_async_copy(stg.at[j], xl.at[pl.ds(seg * chunks, chunks)], ch_r.at[seg]).start()

        @pl.when(jnp.logical_not(own))
        def _():
            push(j).start()

    lo = lax.broadcasted_iota(jnp.int32, (MB, 128), 1) < 64

    def project_role():
        def spread(t, _):
            ct = need_order(t)

            @pl.when(sec == 1)
            def _():
                arrived(hd, ct)
                for k in (2, 1, 3):
                    direct(ct, k).start()

            pass_on(ct, 0).start()
            return 0

        def relay(t, _):
            ct = need_order(t)
            for k in (1, 3, 2):
                arrived(2 * lax.rem(y + k, n_y) + c, ct)
                pass_on(ct, k).start()
            return 0

        def add(k):
            chip = lax.rem(y + k, n_y)

            def await_one(t, _):
                arrived(2 * chip + 1 - c, need_order(t))
                return 0

            lax.fori_loop(0, chunks, await_one, 0)
            h = jnp.concatenate([hbuf[2 * chip], hbuf[2 * chip + 1]], axis=1)
            at = pl.ds(pl.multiple_of(chip * 2 * cols, 128), 2 * cols)
            for i in range(3):
                part = dot(h, inw[i, at])
                acc[i] = part if k == 0 else acc[i] + part

        lax.fori_loop(0, chunks, spread, 0)
        load_in.wait()
        add(0)
        lax.fori_loop(0, chunks, relay, 0)
        for k in (1, 3, 2):
            add(k)

        io0 = lax.broadcasted_iota(jnp.int32, (128, 128), 0) // 64
        io1 = lax.broadcasted_iota(jnp.int32, (128, 128), 1) // 64
        ones = jnp.where(io0 == io1, 1.0 / 64, 0.0).astype(bf)
        live = lax.broadcasted_iota(jnp.int32, (rows, 128), 0) < counts[0]
        lo_all = lax.broadcasted_iota(jnp.int32, (rows, 128), 1) < 64

        def unit_rows(x):
            x = x.astype(bf).astype(f32)
            sq = x * x
            top = sq.astype(bf)
            low = (sq - top.astype(f32)).astype(bf)
            return x * lax.rsqrt(dot(top, ones) + dot(low, ones) + 1e-06)

        for pair in range(heads // 2):
            at = slice(pair * 128, pair * 128 + 128)
            q = unit_rows(acc[0, :, at])
            k = unit_rows(acc[1, :, at])
            v = unit_rows(acc[2, :, at])
            d = jnp.where(live, k - v, 0.0)
            k = jnp.where(live, k, 0.0)
            rolled = pltpu.roll(d, 64, 1)
            even = jnp.where(lo_all, q, pltpu.roll(k, 64, 1)).astype(bf)
            odd = jnp.where(lo_all, pltpu.roll(q, 64, 1), k).astype(bf)
            for ct in range(chunks):
                top = slice(ct * MB, ct * MB + MB // 2)
                bot = slice(ct * MB + MB // 2, ct * MB + MB)
                half_lo = lo[0 : MB // 2]
                stg[2 * pair, ct, 0:64] = even[ct * MB : ct * MB + MB]
                stg[2 * pair, ct, 64:96] = jnp.where(half_lo, d[top], rolled[bot]).astype(bf)
                stg[2 * pair + 1, ct, 0:64] = odd[ct * MB : ct * MB + MB]
                stg[2 * pair + 1, ct, 64:96] = jnp.where(half_lo, rolled[top], d[bot]).astype(bf)

            give(2 * pair)
            give(2 * pair + 1)

    def to_sibling(ct):
        return send(p1.at[ct], rs1.at[ct], rs1_s.at[ct], rs1_r.at[ct], dev(seg, sib, sec))

    def to_chip(ct, k):
        other = lax.rem(y + k, n_y)
        return send(p2.at[ct, k], rs2.at[ct, k], rs2_s.at[k, ct], rs2_r.at[k, ct], dev(seg, 2 * other + c, sec))

    def mix_in(ct, j):
        part = mixb.at[j, span(ct)]
        return send(part, part, mix_s.at[0], mix_r.at[j, ct], dev(seg, sib, sec))

    def columns(head):
        return pl.ds(pl.multiple_of(head * cols, 128), cols)

    def combine_role():
        load_out.wait()

        def multiply(ct):
            for j in range(heads):
                mix_in(ct, j).wait_recv()
            pairs = [mixb[2 * i, span(ct)] + mixb[2 * i + 1, span(ct)] for i in range(heads // 2)]
            mixture = jnp.concatenate(pairs, axis=1)
            for k in range(n_y):
                other = lax.rem(y + k, n_y)
                p1[ct, k] = dot(mixture, outw[:, columns(2 * other + 1 - c)]).astype(bf)
            to_sibling(ct).start()
            for k in range(n_y):
                other = lax.rem(y + k, n_y)
                p2f[ct, k] = dot(mixture, outw[:, columns(2 * other + c)])

        def reduce(ct):
            to_sibling(ct).wait_recv()
            for k in (1, 3, 2):
                p2[ct, k] = (p2f[ct, k] + rs1[ct, k].astype(f32)).astype(bf)
                to_chip(ct, k).start()

        def finish(t, _):
            ct = done_order(t)
            acc = p2f[ct, 0] + rs1[ct, 0].astype(f32)
            for k in (1, 3, 2):
                to_chip(ct, k).wait_recv()
                acc = acc + rs2[ct, k].astype(f32)
            panel[0, span(ct)] = (hbuf[hd, span(ct)].astype(f32) + acc).astype(bf)

            @pl.when(sec == 0)
            def _():
                hop(ct).start()

            return 0

        def two(t, _):
            @pl.when(t < chunks)
            def _():
                multiply(done_order(t))

            @pl.when(t > 0)
            def _():
                reduce(done_order(t - 1))

            return 0

        lax.fori_loop(0, chunks + 1, two, 0)
        lax.fori_loop(0, chunks, finish, 0)

    def at(i):
        return i + c * (nb - 1 - 2 * i)

    def number(g):
        return g + c * (n_seg - 1 - 2 * g)

    def three(g):
        return xl.at[pl.ds(number(g) * chunks, chunks)]

    def forward(g):
        return send(three(g), three(g), fw_s.at[g], ch_r.at[number(g)], dev(seg, sib, sec))

    def landed(g):
        send(three(g), three(g), fw_s.at[0], ch_r.at[number(g)], dev(seg, sib, sec)).wait_recv()

    def exchange(g):
        return send(exs.at[g], exl.at[g], ex_s.at[g], ex_r.at[g], dev(seg, sib, sec))

    def give_back(i):
        b = at(i)
        return send(
            mxs.at[i - half], mixb.at[mine, span(lax.rem(b, chunks))], mix_s.at[i - half],
            mix_r.at[mine, lax.rem(b, chunks)], dev(b // chunks, 2 * y + cg, sec),
        )

    def chain_role():
        ub[...] = jnp.zeros_like(ub)

        @pl.when(jnp.logical_not(holder))
        def _():
            init_send.wait_recv()

        u[...] = ini[0:64]
        ub[64:128] = ini[0:64].astype(bf)
        w0 = jnp.concatenate([jnp.zeros((128, 64), f32), jnp.swapaxes(ini[64:128], 0, 1)], axis=1)
        w[...] = w0
        wk[...] = w0.astype(bf)
        sc = ini[128:129]
        landed(0)
        forward(0).start()

        z = dot(xl[at(0), 0:64], ub[0:128])

        def mixed(m, t, mine_out):
            i = chunks * m + t - 1
            slot = nb + 1 - chunks * m - t
            both = mine_out + exl[slot // chunks, lax.rem(slot, chunks)]
            both = jnp.where(lo, 0.0, both)
            both = jnp.where(lax.rem(mine, 2) == 0, pltpu.roll(both, 64, 1), both)
            mxs[i - half] = both.astype(bf)
            give_back(i).start()

        def group(g, carry):
            @pl.when(g < n_seg - 1)
            def _():
                landed(g + 1)

            @pl.when(g < line - 1)
            def _():
                forward(g + 1).start()

            z, back = carry
            for t in range(chunks):
                i = chunks * g + t
                before, after = jnp.maximum(i - 1, 0), jnp.minimum(i + 1, nb - 1)
                z, back, out = chain_step(xl, at(before), at(i), at(after), z, back, sc, u, w, ub, wk)
                exs[g, t] = out

            @pl.when(g <= line)
            def _():
                exchange(g).start()

            @pl.when(g > line)
            def _():
                m = g - 1

                @pl.when(m == line)
                def _():
                    exchange(line).wait_recv()

                exchange(n_seg - 1 - m).wait_recv()

                @pl.when(m > line)
                def _():
                    mixed(m, 0, exs[m, 0])

                for t in range(1, chunks):
                    mixed(m, t, exs[m, t])

            return z, back

        carry = lax.fori_loop(0, n_seg, group, (z, jnp.zeros((64, 128), bf)))
        exchange(0).wait_recv()
        for t in range(chunks):
            mixed(n_seg - 1, t, exs[n_seg - 1, t])
        last = xl[at(nb - 1), 0:64]
        ub[64:128] = (u[...] - dot_tn(last, carry[1])[64:128]).astype(bf)
        aq = smooth(dot(last, ub[64:192])).astype(bf)
        mixed(n_seg, 0, pltpu.roll(last.astype(f32), 64, 1) + dot(aq, wk[...]))

        def drain(i, _):
            give_back(half + i).wait_send()
            return 0

        lax.fori_loop(0, half, drain, 0)
        for g in range(line):
            forward(g).wait_send()
        for g in range(line + 1):
            exchange(g).wait_send()

    project_role()

    @pl.when(in_chain)
    def _():
        chain_role()

    combine_role()

    def drain(ct, _):
        for k in range(n_y):
            pass_on(ct, k).wait_send()
        for k in range(1, n_y):
            direct(ct, k).wait_send()
            to_chip(ct, k).wait_send()
        to_sibling(ct).wait_send()

        @pl.when(sec == 0)
        def _():
            hop(ct).wait_send()

        return 0

    lax.fori_loop(0, chunks, drain, 0)
    for j in range(heads):

        @pl.when(jnp.logical_not(jnp.logical_and(holder, mine == j)))
        def _():
            push(j).wait_send()

    @pl.when(holder)
    def _():
        init_send.wait_send()


def solution(mesh):
    n_seg, n_head = mesh.shape["seg"], mesh.shape["head"]
    placed = (
        P("seg", "head"),
        P("section", None, None, "head"),
        P("section", "head", None),
        P("section", None, "head", None, None),
        P("section", None, "head", None, None),
        P("section", None, "head"),
        P("seg"),
    )

    def local(tokens, in_weight, out_weight, expand_init, contract_init, inner_rate, seg_counts):
        rows, cols = tokens.shape
        heads = expand_init.shape[2]
        chunks = rows // MB
        nb = n_seg * chunks
        n_y = n_head // 2
        any_space = pl.BlockSpec(memory_space=pltpu.HBM)
        vmem = pl.BlockSpec(memory_space=pltpu.VMEM)
        smem = pl.BlockSpec(memory_space=pltpu.SMEM)
        dma = pltpu.SemaphoreType.DMA
        return pl.pallas_call(
            functools.partial(kernel, n_seg, n_head, heads),
            out_shape=jax.ShapeDtypeStruct((1, rows, cols), bf),
            in_specs=[any_space] * 5 + [vmem, smem],
            out_specs=vmem,
            scratch_shapes=[
                pltpu.VMEM(in_weight.shape[1:], bf),
                pltpu.VMEM(out_weight.shape[1:], bf),
                pltpu.VMEM((n_head, rows, cols), bf),
                pltpu.VMEM((3, rows, cols), f32),
                pltpu.VMEM((heads, chunks, 96, 128), bf),
                pltpu.VMEM((nb, 96, 128), bf),
                pltpu.VMEM((136, 128), f32),
                pltpu.VMEM((136, 128), f32),
                pltpu.VMEM((n_seg, chunks, 64, 128), f32),
                pltpu.VMEM((n_seg // 2 + 1, chunks, 64, 128), f32),
                pltpu.VMEM((nb // 2, 64, 128), bf),
                pltpu.VMEM((heads, rows, 128), bf),
                pltpu.VMEM((chunks, n_y, MB, cols), bf),
                pltpu.VMEM((chunks, n_y, MB, cols), f32),
                pltpu.VMEM((chunks, n_y, MB, cols), bf),
                pltpu.VMEM((chunks, n_y, MB, cols), bf),
                pltpu.VMEM((chunks, n_y, MB, cols), bf),
                pltpu.VMEM((64, 128), f32),
                pltpu.VMEM((128, 128), f32),
                pltpu.VMEM((192, 128), bf),
                pltpu.VMEM((128, 128), bf),
                dma((2,)),
                dma,
                dma((4,)),
                dma((n_y, chunks)),
                dma((n_head, chunks)),
                dma((n_y, chunks)),
                dma((chunks,)),
                dma((heads,)),
                dma((n_seg,)),
                dma((n_seg // 2,)),
                dma((n_seg // 2 + 1,)),
                dma((n_seg // 2 + 1,)),
                dma((nb // 2,)),
                dma((heads, chunks)),
                dma((chunks,)),
                dma((chunks,)),
                dma((n_y, chunks)),
                dma((n_y, chunks)),
                dma,
                dma,
            ],
            compiler_params=pltpu.CompilerParams(
                collective_id=0, has_side_effects=True, vmem_limit_bytes=60 << 20
            ),
            name="both_groups",
        )(tokens, in_weight, out_weight, expand_init, jnp.swapaxes(contract_init, 3, 4), inner_rate, seg_counts)

    return jax.shard_map(
        local, mesh=mesh, in_specs=placed, out_specs=P("section", "seg", "head"), check_vma=False
    )
```

```python
import functools
import math

import jax
import jax.numpy as jnp
from jax import lax
from jax.experimental import pallas as pl
from jax.experimental.pallas import tpu as pltpu
from jax.sharding import PartitionSpec as P

MB = 64
C1 = math.sqrt(2.0 / math.pi)
C3 = 0.044715
f32 = jnp.float32
bf = jnp.bfloat16


def dot(a, b):
    return lax.dot_general(a, b, (((1,), (0,)), ((), ())), preferred_element_type=f32)


def dot_nt(a, b):
    return lax.dot_general(a, b, (((1,), (1,)), ((), ())), preferred_element_type=f32)


def dot_tn(a, b):
    return lax.dot_general(a, b, (((0,), (0,)), ((), ())), preferred_element_type=f32)


def smooth(z):
    t = jnp.tanh(z * (C1 + (C1 * C3) * (z * z)))
    h = 0.5 * z
    return h + h * t


def smooth_slope(z):
    z2 = z * z
    t = jnp.tanh(z * (C1 + (C1 * C3) * z2))
    h = 0.5 * z
    return h + h * t, 0.5 + 0.5 * t + h * (1.0 - t * t) * (C1 + (3.0 * C1 * C3) * z2)


def chain_step(xl, bp, b, bn, z, bk, sc, u, w, ub, wk):
    xp, xb, xn = xl[bp, 0:64], xl[b, 0:64], xl[bn, 0:64]
    dp = xl[b, 64:96].astype(f32)
    hi = lax.broadcasted_iota(jnp.int32, (64, 128), 1) >= 64
    a, s = smooth_slope(z)
    s = s * sc
    ab = a.astype(bf)
    wkv = wk[...]
    delta = jnp.where(hi, jnp.concatenate([pltpu.roll(dp, 64, 1), dp], 0), 0.0)
    e = delta + dot(ab, wkv)
    back = (dot_nt(e.astype(bf), wkv) * s).astype(bf)
    un = u[...] - dot_tn(xp, bk)[64:128]
    u[...] = un
    ub[64:128] = un.astype(bf)
    zq = dot(xp, ub[64:192])
    gram = dot_nt(jnp.where(hi, xn, jnp.zeros_like(xn)), xb).astype(bf)
    zn = dot(xn, ub[0:128]) - dot(gram, back)
    aq = smooth(zq).astype(bf)
    out = pltpu.roll(xp.astype(f32), 64, 1) + dot(aq, wkv)
    wn = w[...] - dot_tn(ab, (e * sc).astype(bf))
    w[...] = wn
    wk[...] = wn.astype(bf)
    return zn, back, out


def kernel(
    n_seg, n_head, heads,
    tokens, in_w, out_w, expand, contract, rate, counts,
    panel,
    inw, outw, hbuf, acc, stg, xl, ini_s, ini, exs, exl, mxs, mixb,
    p1, p2f, rs1, p2, rs2, u, w, ub, wk,
    wsem, tsem, isem, ag_s, ag_r, po_s, hop_s, push_s, ch_r, fw_s, fw_r, ex_s, ex_r,
    mix_s, mix_r, rs1_s, rs1_r, rs2_s, rs2_r, ini_ss, ini_r,
):
    rows = tokens.shape[0]
    cols = tokens.shape[1]
    chunks = rows // MB
    nb = n_seg * chunks
    half = nb // 2
    n_y = n_head // 2
    line = n_seg // 2
    turn_by = line // 2 + 1
    sec = lax.axis_index("section")
    seg = lax.axis_index("seg")
    hd = lax.axis_index("head")
    y = hd // 2
    c = lax.rem(hd, 2)
    sib = 2 * y + 1 - c
    late = seg // line
    spot = lax.rem(lax.rem(seg, line) + line - turn_by, line)
    in_chain = spot < heads
    cg = late
    mine = jnp.minimum(spot, heads - 1)

    def place(group, j):
        return group * line + lax.rem(j + turn_by, line)

    holder = jnp.logical_and(in_chain, cg == c)

    def dev(s, h, x):
        return {"seg": s, "head": h, "section": x}

    def send(src, dst, s_sem, r_sem, device):
        return pltpu.make_async_remote_copy(
            src_ref=src, dst_ref=dst, send_sem=s_sem, recv_sem=r_sem,
            device_id=device, device_id_type=pl.DeviceIdType.MESH,
        )

    def span(ct):
        return pl.ds(pl.multiple_of(ct * MB, MB), MB)

    load_in = pltpu.make_async_copy(in_w.at[0], inw, wsem.at[0])
    load_out = pltpu.make_async_copy(out_w.at[0], outw, wsem.at[1])
    load_tok = pltpu.make_async_copy(tokens, hbuf.at[hd], tsem)

    @pl.when(sec == 0)
    def _():
        load_tok.start()

    load_in.start()
    load_out.start()

    barrier = pltpu.get_barrier_semaphore()

    def greet(device):
        pl.semaphore_signal(barrier, inc=1, device_id=device, device_id_type=pl.DeviceIdType.MESH)

    for j in range(heads):
        greet(dev(place(c, j), 2 * y + 1 - late, sec))

    @pl.when(in_chain)
    def _():
        for k in range(line):
            source = c * line + k

            @pl.when(jnp.logical_not(jnp.logical_and(holder, source == seg)))
            def _():
                greet(dev(source, 2 * y + cg, sec))

    @pl.when(sec == 1)
    def _():
        greet(dev(seg, hd, 0))

    for k in range(1, n_head):
        greet(dev(seg, lax.rem(hd + k, n_head), sec))

    @pl.when(holder)
    def _():
        loads = []
        for way, to in ((c, ini), (1 - c, ini_s)):
            loads.append(pltpu.make_async_copy(expand.at[0, way, mine], to.at[pl.ds(0, 64)], isem.at[len(loads)]))
            loads.append(pltpu.make_async_copy(contract.at[0, way, mine], to.at[pl.ds(64, 64)], isem.at[len(loads)]))
        for copy in loads:
            copy.start()
        every = rate[0]
        at_way = lax.broadcasted_iota(jnp.int32, every.shape, 0)
        at_head = lax.broadcasted_iota(jnp.int32, every.shape, 1)
        for way, to in ((c, ini), (1 - c, ini_s)):
            picked = jnp.where((at_way == way) & (at_head == mine), every, 0.0)
            one = jnp.sum(picked, axis=(0, 1), keepdims=True) * (1.0 / (64 * MB))
            to[128:136] = jnp.broadcast_to(one, (8, 128))
        for copy in loads:
            copy.wait()

    @pl.when(sec == 0)
    def _():
        load_tok.wait()

    total = n_head - 1 + heads + (1 - sec)
    total = total + jnp.where(in_chain, line, 0) - jnp.where(holder, 1, 0)
    pl.semaphore_wait(barrier, total)

    def direct(ct, k):
        part = hbuf.at[hd, span(ct)]
        return send(part, part, ag_s.at[k, ct], ag_r.at[hd, ct], dev(seg, 2 * lax.rem(y + k, n_y) + c, sec))

    def hop(ct):
        return send(panel.at[0, span(ct)], hbuf.at[hd, span(ct)], hop_s.at[ct], ag_r.at[hd, ct], dev(seg, hd, 1))

    def pass_on(ct, k):
        slot = 2 * lax.rem(y + k, n_y) + c
        part = hbuf.at[slot, span(ct)]
        return send(part, part, po_s.at[k, ct], ag_r.at[slot, ct], dev(seg, sib, sec))

    def arrived(slot, ct):
        part = hbuf.at[slot, span(ct)]
        send(part, part, po_s.at[0, ct], ag_r.at[slot, ct], dev(seg, sib, sec)).wait_recv()

    flip = lax.rem(late + sec, 2)

    def need_order(t):
        return t + flip * (chunks - 1 - 2 * t)

    def done_order(t):
        return t + (1 - late) * (chunks - 1 - 2 * t)

    @pl.when(sec == 0)
    def _():
        def go(t, _):
            for k in (2, 1, 3):
                direct(need_order(t), k).start()
            return 0

        lax.fori_loop(0, chunks, go, 0)

    init_send = send(ini_s, ini, ini_ss, ini_r, dev(seg, sib, sec))

    @pl.when(holder)
    def _():
        init_send.start()

    part_first = (flip * (chunks - 1), 1 - flip)
    part_size = (1, chunks - 1)

    def block(p):
        return pl.ds(seg * chunks + part_first[p], part_size[p])

    def push(j, p):
        return send(
            stg.at[j, pl.ds(part_first[p], part_size[p])], xl.at[block(p)], push_s.at[j, p], ch_r.at[seg, p],
            dev(place(c, j), 2 * y + late, sec),
        )

    def give(j, p):
        own = jnp.logical_and(holder, mine == j)

        @pl.when(own)
        def _():
            pltpu.make_async_copy(
                stg.at[j, pl.ds(part_first[p], part_size[p])], xl.at[block(p)], ch_r.at[seg, p]
            ).start()

        @pl.when(jnp.logical_not(own))
        def _():
            push(j, p).start()

    lo = lax.broadcasted_iota(jnp.int32, (MB, 128), 1) < 64

    def project_role():
        io0 = lax.broadcasted_iota(jnp.int32, (128, 128), 0) // 64
        io1 = lax.broadcasted_iota(jnp.int32, (128, 128), 1) // 64
        ones = jnp.where(io0 == io1, 1.0 / 64, 0.0).astype(bf)

        def unit_rows(x):
            x = x.astype(bf).astype(f32)
            sq = x * x
            top = sq.astype(bf)
            low = (sq - top.astype(f32)).astype(bf)
            return x * lax.rsqrt(dot(top, ones) + dot(low, ones) + 1e-06)

        def spread(t, _):
            ct = need_order(t)

            @pl.when(sec == 1)
            def _():
                arrived(hd, ct)
                for k in (2, 1, 3):
                    direct(ct, k).start()

            pass_on(ct, 0).start()
            return 0

        def relay(t, _):
            ct = need_order(t)
            for k in (1, 3, 2):
                arrived(2 * lax.rem(y + k, n_y) + c, ct)
                pass_on(ct, k).start()
            return 0

        def part(p):
            times = (0, 1) if p == 0 else (1, chunks)
            size = part_size[p] * MB
            begin = pl.multiple_of(part_first[p] * MB, MB)
            span_p = pl.ds(begin, size)

            def add(k):
                chip = lax.rem(y + k, n_y)

                def await_one(t, _):
                    arrived(2 * chip + 1 - c, need_order(t))
                    return 0

                lax.fori_loop(*times, await_one, 0)
                h = jnp.concatenate([hbuf[2 * chip, span_p], hbuf[2 * chip + 1, span_p]], axis=1)
                at = pl.ds(pl.multiple_of(chip * 2 * cols, 128), 2 * cols)
                for i in range(3):
                    term = dot(h, inw[i, at])
                    acc[i, 0:size] = term if k == 0 else acc[i, 0:size] + term

            if p == 0:
                lax.fori_loop(*times, spread, 0)
                load_in.wait()
                add(0)
                lax.fori_loop(*times, relay, 0)
                lax.fori_loop(1, chunks, spread, 0)
            else:
                add(0)
                lax.fori_loop(*times, relay, 0)
            for k in (1, 3, 2):
                add(k)
            live = lax.broadcasted_iota(jnp.int32, (size, 128), 0) + begin < counts[0]
            lo_all = lax.broadcasted_iota(jnp.int32, (size, 128), 1) < 64
            for pair in range(heads // 2):
                at = slice(pair * 128, pair * 128 + 128)
                q = unit_rows(acc[0, 0:size, at])
                k = unit_rows(acc[1, 0:size, at])
                v = unit_rows(acc[2, 0:size, at])
                d = jnp.where(live, k - v, 0.0)
                k = jnp.where(live, k, 0.0)
                rolled = pltpu.roll(d, 64, 1)
                even = jnp.where(lo_all, q, pltpu.roll(k, 64, 1)).astype(bf)
                odd = jnp.where(lo_all, pltpu.roll(q, 64, 1), k).astype(bf)
                half_lo = lo[0 : MB // 2]
                for n in range(part_size[p]):
                    ct = part_first[p] + n
                    top = slice(n * MB, n * MB + MB // 2)
                    bot = slice(n * MB + MB // 2, n * MB + MB)
                    stg[2 * pair, ct, 0:64] = even[n * MB : n * MB + MB]
                    stg[2 * pair, ct, 64:96] = jnp.where(half_lo, d[top], rolled[bot]).astype(bf)
                    stg[2 * pair + 1, ct, 0:64] = odd[n * MB : n * MB + MB]
                    stg[2 * pair + 1, ct, 64:96] = jnp.where(half_lo, rolled[top], d[bot]).astype(bf)
                give(2 * pair, p)
                give(2 * pair + 1, p)

        part(0)
        part(1)

    def to_sibling(ct):
        return send(p1.at[ct], rs1.at[ct], rs1_s.at[ct], rs1_r.at[ct], dev(seg, sib, sec))

    def to_chip(ct, k):
        other = lax.rem(y + k, n_y)
        return send(p2.at[ct, k], rs2.at[ct, k], rs2_s.at[k, ct], rs2_r.at[k, ct], dev(seg, 2 * other + c, sec))

    def mix_in(ct, j):
        part = mixb.at[j, span(ct)]
        return send(part, part, mix_s.at[0], mix_r.at[j, ct], dev(seg, sib, sec))

    def columns(head):
        return pl.ds(pl.multiple_of(head * cols, 128), cols)

    def combine_role():
        load_out.wait()

        def multiply(ct):
            for j in range(heads):
                mix_in(ct, j).wait_recv()
            pairs = [mixb[2 * i, span(ct)] + mixb[2 * i + 1, span(ct)] for i in range(heads // 2)]
            mixture = jnp.concatenate(pairs, axis=1)
            for k in range(n_y):
                other = lax.rem(y + k, n_y)
                p1[ct, k] = dot(mixture, outw[:, columns(2 * other + 1 - c)]).astype(bf)
            to_sibling(ct).start()
            for k in range(n_y):
                other = lax.rem(y + k, n_y)
                p2f[ct, k] = dot(mixture, outw[:, columns(2 * other + c)])

        def reduce(ct):
            to_sibling(ct).wait_recv()
            for k in (1, 3, 2):
                p2[ct, k] = (p2f[ct, k] + rs1[ct, k].astype(f32)).astype(bf)
                to_chip(ct, k).start()

        def finish(t, _):
            ct = done_order(t)
            acc = p2f[ct, 0] + rs1[ct, 0].astype(f32)
            for k in (1, 3, 2):
                to_chip(ct, k).wait_recv()
                acc = acc + rs2[ct, k].astype(f32)
            panel[0, span(ct)] = (hbuf[hd, span(ct)].astype(f32) + acc).astype(bf)

            @pl.when(sec == 0)
            def _():
                hop(ct).start()

            return 0

        def two(t, _):
            @pl.when(t < chunks)
            def _():
                multiply(done_order(t))

            @pl.when(t > 0)
            def _():
                reduce(done_order(t - 1))

            return 0

        lax.fori_loop(0, chunks + 1, two, 0)
        lax.fori_loop(0, chunks, finish, 0)

    def at(i):
        return i + c * (nb - 1 - 2 * i)

    def number(g):
        return g + c * (n_seg - 1 - 2 * g)

    def three(g):
        return xl.at[pl.ds(number(g) * chunks, chunks)]

    def forward(g):
        return send(three(g), three(g), fw_s.at[g], fw_r.at[number(g)], dev(seg, sib, sec))

    def landed(g):
        send(three(g), three(g), fw_s.at[0], fw_r.at[number(g)], dev(seg, sib, sec)).wait_recv()

    def came(g, p):
        turned = lax.rem(c + sec, 2)
        begin = (turned * (chunks - 1), 1 - turned)[p]
        here = xl.at[pl.ds(number(g) * chunks + begin, part_size[p])]
        send(here, here, fw_s.at[0], ch_r.at[number(g), p], dev(seg, sib, sec)).wait_recv()

    def exchange(g):
        return send(exs.at[g], exl.at[g], ex_s.at[g], ex_r.at[g], dev(seg, sib, sec))

    def give_back(i):
        b = at(i)
        return send(
            mxs.at[i - half], mixb.at[mine, span(lax.rem(b, chunks))], mix_s.at[i - half],
            mix_r.at[mine, lax.rem(b, chunks)], dev(b // chunks, 2 * y + cg, sec),
        )

    def chain_role():
        ub[...] = jnp.zeros_like(ub)

        @pl.when(jnp.logical_not(holder))
        def _():
            init_send.wait_recv()

        u[...] = ini[0:64]
        ub[64:128] = ini[0:64].astype(bf)
        w0 = jnp.concatenate([jnp.zeros((128, 64), f32), jnp.swapaxes(ini[64:128], 0, 1)], axis=1)
        w[...] = w0
        wk[...] = w0.astype(bf)
        sc = ini[128:129]
        came(0, 0)

        @pl.when(sec == 1)
        def _():
            came(0, 1)
            forward(0).start()


        z = dot(xl[at(0), 0:64], ub[0:128])

        def mixed(m, t, mine_out):
            i = chunks * m + t - 1
            slot = nb + 1 - chunks * m - t
            both = mine_out + exl[slot // chunks, lax.rem(slot, chunks)]
            both = jnp.where(lo, 0.0, both)
            both = jnp.where(lax.rem(mine, 2) == 0, pltpu.roll(both, 64, 1), both)
            mxs[i - half] = both.astype(bf)
            give_back(i).start()

        def group(g, carry):
            ahead = jnp.where(sec == 1, 0, line // 2 - 1)

            @pl.when(jnp.logical_and(g <= ahead, sec == 0))
            def _():
                came(g, 1)
                forward(g).start()

            @pl.when(g < line - 1)
            def _():
                came(g + 1, 0)

            @pl.when(jnp.logical_and(g >= ahead, g < line - 1))
            def _():
                came(g + 1, 1)
                forward(g + 1).start()

            @pl.when(jnp.logical_and(g >= line - 1, g < n_seg - 1))
            def _():
                landed(g + 1)

            z, back = carry
            for t in range(chunks):
                i = chunks * g + t
                before, after = jnp.maximum(i - 1, 0), jnp.minimum(i + 1, nb - 1)
                z, back, out = chain_step(xl, at(before), at(i), at(after), z, back, sc, u, w, ub, wk)
                exs[g, t] = out

            @pl.when(g <= line)
            def _():
                exchange(g).start()

            @pl.when(g > line)
            def _():
                m = g - 1

                @pl.when(m == line)
                def _():
                    exchange(line).wait_recv()

                exchange(n_seg - 1 - m).wait_recv()

                @pl.when(m > line)
                def _():
                    mixed(m, 0, exs[m, 0])

                for t in range(1, chunks):
                    mixed(m, t, exs[m, t])

            return z, back

        carry = lax.fori_loop(0, n_seg, group, (z, jnp.zeros((64, 128), bf)))
        exchange(0).wait_recv()
        for t in range(chunks):
            mixed(n_seg - 1, t, exs[n_seg - 1, t])
        last = xl[at(nb - 1), 0:64]
        ub[64:128] = (u[...] - dot_tn(last, carry[1])[64:128]).astype(bf)
        aq = smooth(dot(last, ub[64:192])).astype(bf)
        mixed(n_seg, 0, pltpu.roll(last.astype(f32), 64, 1) + dot(aq, wk[...]))

    def chain_drain():
        def drain(i, _):
            give_back(half + i).wait_send()
            return 0

        lax.fori_loop(0, half, drain, 0)
        for g in range(line):
            forward(g).wait_send()
        for g in range(line + 1):
            exchange(g).wait_send()

    project_role()

    @pl.when(in_chain)
    def _():
        chain_role()

    combine_role()

    def drain(ct, _):
        for k in range(n_y):
            pass_on(ct, k).wait_send()
        for k in range(1, n_y):
            direct(ct, k).wait_send()
            to_chip(ct, k).wait_send()
        to_sibling(ct).wait_send()

        @pl.when(sec == 0)
        def _():
            hop(ct).wait_send()

        return 0

    lax.fori_loop(0, chunks, drain, 0)

    @pl.when(in_chain)
    def _():
        chain_drain()

    for j in range(heads):

        @pl.when(jnp.logical_not(jnp.logical_and(holder, mine == j)))
        def _():
            for p in range(2):
                push(j, p).wait_send()

    @pl.when(holder)
    def _():
        init_send.wait_send()


def solution(mesh):
    n_seg, n_head = mesh.shape["seg"], mesh.shape["head"]
    placed = (
        P("seg", "head"),
        P("section", None, None, "head"),
        P("section", "head", None),
        P("section", None, "head", None, None),
        P("section", None, "head", None, None),
        P("section", None, "head"),
        P("seg"),
    )

    def local(tokens, in_weight, out_weight, expand_init, contract_init, inner_rate, seg_counts):
        rows, cols = tokens.shape
        heads = expand_init.shape[2]
        chunks = rows // MB
        nb = n_seg * chunks
        n_y = n_head // 2
        any_space = pl.BlockSpec(memory_space=pltpu.HBM)
        vmem = pl.BlockSpec(memory_space=pltpu.VMEM)
        smem = pl.BlockSpec(memory_space=pltpu.SMEM)
        dma = pltpu.SemaphoreType.DMA
        return pl.pallas_call(
            functools.partial(kernel, n_seg, n_head, heads),
            out_shape=jax.ShapeDtypeStruct((1, rows, cols), bf),
            in_specs=[any_space] * 5 + [vmem, smem],
            out_specs=vmem,
            scratch_shapes=[
                pltpu.VMEM(in_weight.shape[1:], bf),
                pltpu.VMEM(out_weight.shape[1:], bf),
                pltpu.VMEM((n_head, rows, cols), bf),
                pltpu.VMEM((3, rows, cols), f32),
                pltpu.VMEM((heads, chunks, 96, 128), bf),
                pltpu.VMEM((nb, 96, 128), bf),
                pltpu.VMEM((136, 128), f32),
                pltpu.VMEM((136, 128), f32),
                pltpu.VMEM((n_seg, chunks, 64, 128), f32),
                pltpu.VMEM((n_seg // 2 + 1, chunks, 64, 128), f32),
                pltpu.VMEM((nb // 2, 64, 128), bf),
                pltpu.VMEM((heads, rows, 128), bf),
                pltpu.VMEM((chunks, n_y, MB, cols), bf),
                pltpu.VMEM((chunks, n_y, MB, cols), f32),
                pltpu.VMEM((chunks, n_y, MB, cols), bf),
                pltpu.VMEM((chunks, n_y, MB, cols), bf),
                pltpu.VMEM((chunks, n_y, MB, cols), bf),
                pltpu.VMEM((64, 128), f32),
                pltpu.VMEM((128, 128), f32),
                pltpu.VMEM((192, 128), bf),
                pltpu.VMEM((128, 128), bf),
                dma((2,)),
                dma,
                dma((4,)),
                dma((n_y, chunks)),
                dma((n_head, chunks)),
                dma((n_y, chunks)),
                dma((chunks,)),
                dma((heads, 2)),
                dma((n_seg, 2)),
                dma((n_seg // 2,)),
                dma((n_seg,)),
                dma((n_seg // 2 + 1,)),
                dma((n_seg // 2 + 1,)),
                dma((nb // 2,)),
                dma((heads, chunks)),
                dma((chunks,)),
                dma((chunks,)),
                dma((n_y, chunks)),
                dma((n_y, chunks)),
                dma,
                dma,
            ],
            compiler_params=pltpu.CompilerParams(
                collective_id=0, has_side_effects=True, vmem_limit_bytes=60 << 20
            ),
            name="both_groups",
        )(tokens, in_weight, out_weight, expand_init, jnp.swapaxes(contract_init, 3, 4), inner_rate, seg_counts)

    return jax.shard_map(
        local, mesh=mesh, in_specs=placed, out_specs=P("section", "seg", "head"), check_vma=False
    )
```

```python
import functools
import math

import jax
import jax.numpy as jnp
from jax import lax
from jax.experimental import pallas as pl
from jax.experimental.pallas import tpu as pltpu
from jax.sharding import PartitionSpec as P

MB = 64
C1 = math.sqrt(2.0 / math.pi)
C3 = 0.044715
f32 = jnp.float32
bf = jnp.bfloat16


def dot(a, b):
    return lax.dot_general(a, b, (((1,), (0,)), ((), ())), preferred_element_type=f32)


def dot_nt(a, b):
    return lax.dot_general(a, b, (((1,), (1,)), ((), ())), preferred_element_type=f32)


def dot_tn(a, b):
    return lax.dot_general(a, b, (((0,), (0,)), ((), ())), preferred_element_type=f32)


def smooth(z):
    t = jnp.tanh(z * (C1 + (C1 * C3) * (z * z)))
    h = 0.5 * z
    return h + h * t


def smooth_slope(z):
    z2 = z * z
    t = jnp.tanh(z * (C1 + (C1 * C3) * z2))
    h = 0.5 * z
    return h + h * t, 0.5 + 0.5 * t + h * (1.0 - t * t) * (C1 + (3.0 * C1 * C3) * z2)


def chain_step(xl, bp, b, bn, z, bk, sc, u, w, ub, wk):
    xp, xb, xn = xl[bp, 0:64], xl[b, 0:64], xl[bn, 0:64]
    dp = xl[b, 64:96].astype(f32)
    hi = lax.broadcasted_iota(jnp.int32, (64, 128), 1) >= 64
    a, s = smooth_slope(z)
    s = s * sc
    ab = a.astype(bf)
    wkv = wk[...]
    delta = jnp.where(hi, jnp.concatenate([pltpu.roll(dp, 64, 1), dp], 0), 0.0)
    e = delta + dot(ab, wkv)
    back = (dot_nt(e.astype(bf), wkv) * s).astype(bf)
    un = u[...] - dot_tn(xp, bk)[64:128]
    u[...] = un
    ub[64:128] = un.astype(bf)
    zq = dot(xp, ub[64:192])
    gram = dot_nt(jnp.where(hi, xn, jnp.zeros_like(xn)), xb).astype(bf)
    zn = dot(xn, ub[0:128]) - dot(gram, back)
    aq = smooth(zq).astype(bf)
    out = pltpu.roll(xp.astype(f32), 64, 1) + dot(aq, wkv)
    wn = w[...] - dot_tn(ab, (e * sc).astype(bf))
    w[...] = wn
    wk[...] = wn.astype(bf)
    return zn, back, out


def kernel(
    n_seg, n_head, heads,
    tokens, in_w, out_w, expand, contract, rate, counts,
    panel,
    inw, outw, hbuf, acc, stg, xl, ini_s, ini, exs, exl, mxs, mixb,
    p1, p2f, rs1, p2, rs2, u, w, ub, wk,
    wsem, tsem, isem, ag_s, ag_r, po_s, hop_s, push_s, ch_r, fw_s, fw_r, ex_s, ex_r,
    mix_s, mix_r, rs1_s, rs1_r, rs2_s, rs2_r, ini_ss, ini_r,
):
    rows = tokens.shape[0]
    cols = tokens.shape[1]
    chunks = rows // MB
    nb = n_seg * chunks
    half = nb // 2
    n_y = n_head // 2
    line = n_seg // 2
    turn_by = line // 2 + 1
    sec = lax.axis_index("section")
    seg = lax.axis_index("seg")
    hd = lax.axis_index("head")
    y = hd // 2
    c = lax.rem(hd, 2)
    sib = 2 * y + 1 - c
    late = seg // line
    spot = lax.rem(lax.rem(seg, line) + line - turn_by, line)
    in_chain = spot < heads
    cg = late
    mine = jnp.minimum(spot, heads - 1)

    def place(group, j):
        return group * line + lax.rem(j + turn_by, line)

    holder = jnp.logical_and(in_chain, cg == c)

    def dev(s, h, x):
        return {"seg": s, "head": h, "section": x}

    def send(src, dst, s_sem, r_sem, device):
        return pltpu.make_async_remote_copy(
            src_ref=src, dst_ref=dst, send_sem=s_sem, recv_sem=r_sem,
            device_id=device, device_id_type=pl.DeviceIdType.MESH,
        )

    def span(ct):
        return pl.ds(pl.multiple_of(ct * MB, MB), MB)

    load_in = pltpu.make_async_copy(in_w.at[0], inw, wsem.at[0])
    load_out = pltpu.make_async_copy(out_w.at[0], outw, wsem.at[1])
    load_tok = pltpu.make_async_copy(tokens, hbuf.at[hd], tsem)

    @pl.when(sec == 0)
    def _():
        load_tok.start()

    load_in.start()
    load_out.start()

    barrier = pltpu.get_barrier_semaphore()

    def greet(device):
        pl.semaphore_signal(barrier, inc=1, device_id=device, device_id_type=pl.DeviceIdType.MESH)

    for j in range(heads):
        greet(dev(place(c, j), 2 * y + 1 - late, sec))

    @pl.when(in_chain)
    def _():
        for k in range(line):
            source = c * line + k

            @pl.when(jnp.logical_not(jnp.logical_and(holder, source == seg)))
            def _():
                greet(dev(source, 2 * y + cg, sec))

    @pl.when(sec == 1)
    def _():
        greet(dev(seg, hd, 0))

    for k in range(1, n_head):
        greet(dev(seg, lax.rem(hd + k, n_head), sec))

    @pl.when(holder)
    def _():
        loads = []
        for way, to in ((c, ini), (1 - c, ini_s)):
            loads.append(pltpu.make_async_copy(expand.at[0, way, mine], to.at[pl.ds(0, 64)], isem.at[len(loads)]))
            loads.append(pltpu.make_async_copy(contract.at[0, way, mine], to.at[pl.ds(64, 64)], isem.at[len(loads)]))
        for copy in loads:
            copy.start()
        for way, to in ((c, ini), (1 - c, ini_s)):
            to[128:136] = jnp.full((8, 128), rate[0, way, mine] * (1.0 / (64 * MB)), f32)
        for copy in loads:
            copy.wait()

    @pl.when(sec == 0)
    def _():
        load_tok.wait()

    total = n_head - 1 + heads + (1 - sec)
    total = total + jnp.where(in_chain, line, 0) - jnp.where(holder, 1, 0)
    pl.semaphore_wait(barrier, total)

    def direct(ct, k):
        part = hbuf.at[hd, span(ct)]
        return send(part, part, ag_s.at[k, ct], ag_r.at[hd, ct], dev(seg, 2 * lax.rem(y + k, n_y) + c, sec))

    def hop(ct):
        return send(panel.at[0, span(ct)], hbuf.at[hd, span(ct)], hop_s.at[ct], ag_r.at[hd, ct], dev(seg, hd, 1))

    def pass_on(ct, k):
        slot = 2 * lax.rem(y + k, n_y) + c
        part = hbuf.at[slot, span(ct)]
        return send(part, part, po_s.at[k, ct], ag_r.at[slot, ct], dev(seg, sib, sec))

    def arrived(slot, ct):
        part = hbuf.at[slot, span(ct)]
        send(part, part, po_s.at[0, ct], ag_r.at[slot, ct], dev(seg, sib, sec)).wait_recv()

    flip = lax.rem(late + sec, 2)

    def need_order(t):
        return t + flip * (chunks - 1 - 2 * t)

    def done_order(t):
        return t + (1 - late) * (chunks - 1 - 2 * t)

    @pl.when(sec == 0)
    def _():
        def go(t, _):
            for k in (2, 1, 3):
                direct(need_order(t), k).start()
            return 0

        lax.fori_loop(0, chunks, go, 0)

    init_send = send(ini_s, ini, ini_ss, ini_r, dev(seg, sib, sec))

    @pl.when(holder)
    def _():
        init_send.start()

    part_first = (flip * (chunks - 1), 1 - flip)
    part_size = (1, chunks - 1)

    def block(p):
        return pl.ds(seg * chunks + part_first[p], part_size[p])

    def push(j, p):
        return send(
            stg.at[j, pl.ds(part_first[p], part_size[p])], xl.at[block(p)], push_s.at[j, p], ch_r.at[seg, p],
            dev(place(c, j), 2 * y + late, sec),
        )

    def give(j, p):
        own = jnp.logical_and(holder, mine == j)

        @pl.when(own)
        def _():
            pltpu.make_async_copy(
                stg.at[j, pl.ds(part_first[p], part_size[p])], xl.at[block(p)], ch_r.at[seg, p]
            ).start()

        @pl.when(jnp.logical_not(own))
        def _():
            push(j, p).start()

    lo = lax.broadcasted_iota(jnp.int32, (MB, 128), 1) < 64

    def project_role():
        io0 = lax.broadcasted_iota(jnp.int32, (128, 128), 0) // 64
        io1 = lax.broadcasted_iota(jnp.int32, (128, 128), 1) // 64
        ones = jnp.where(io0 == io1, 1.0 / 64, 0.0).astype(bf)

        def unit_rows(x):
            x = x.astype(bf).astype(f32)
            sq = x * x
            top = sq.astype(bf)
            low = (sq - top.astype(f32)).astype(bf)
            return x * lax.rsqrt(dot(top, ones) + dot(low, ones) + 1e-06)

        def spread(t, _):
            ct = need_order(t)

            @pl.when(sec == 1)
            def _():
                arrived(hd, ct)
                for k in (2, 1, 3):
                    direct(ct, k).start()

            pass_on(ct, 0).start()
            return 0

        def relay(t, _):
            ct = need_order(t)
            for k in (1, 3, 2):
                arrived(2 * lax.rem(y + k, n_y) + c, ct)
                pass_on(ct, k).start()
            return 0

        def part(p):
            times = (0, 1) if p == 0 else (1, chunks)
            size = part_size[p] * MB
            begin = pl.multiple_of(part_first[p] * MB, MB)
            span_p = pl.ds(begin, size)

            def add(k):
                chip = lax.rem(y + k, n_y)

                def await_one(t, _):
                    arrived(2 * chip + 1 - c, need_order(t))
                    return 0

                lax.fori_loop(*times, await_one, 0)
                h = jnp.concatenate([hbuf[2 * chip, span_p], hbuf[2 * chip + 1, span_p]], axis=1)
                at = pl.ds(pl.multiple_of(chip * 2 * cols, 128), 2 * cols)
                for i in range(3):
                    term = dot(h, inw[i, at])
                    acc[i, 0:size] = term if k == 0 else acc[i, 0:size] + term

            if p == 0:
                lax.fori_loop(0, chunks, spread, 0)
                load_in.wait()
                add(0)
                relay(0, 0)
            else:
                relay(1, 0)
                add(0)
                lax.fori_loop(2, chunks, relay, 0)
            for k in (1, 3, 2):
                add(k)
            live = lax.broadcasted_iota(jnp.int32, (size, 128), 0) + begin < counts[0]
            lo_all = lax.broadcasted_iota(jnp.int32, (size, 128), 1) < 64
            for pair in range(heads // 2):
                at = slice(pair * 128, pair * 128 + 128)
                q = unit_rows(acc[0, 0:size, at])
                k = unit_rows(acc[1, 0:size, at])
                v = unit_rows(acc[2, 0:size, at])
                d = jnp.where(live, k - v, 0.0)
                k = jnp.where(live, k, 0.0)
                rolled = pltpu.roll(d, 64, 1)
                even = jnp.where(lo_all, q, pltpu.roll(k, 64, 1)).astype(bf)
                odd = jnp.where(lo_all, pltpu.roll(q, 64, 1), k).astype(bf)
                half_lo = lo[0 : MB // 2]
                for n in range(part_size[p]):
                    ct = part_first[p] + n
                    top = slice(n * MB, n * MB + MB // 2)
                    bot = slice(n * MB + MB // 2, n * MB + MB)
                    stg[2 * pair, ct, 0:64] = even[n * MB : n * MB + MB]
                    stg[2 * pair, ct, 64:96] = jnp.where(half_lo, d[top], rolled[bot]).astype(bf)
                    stg[2 * pair + 1, ct, 0:64] = odd[n * MB : n * MB + MB]
                    stg[2 * pair + 1, ct, 64:96] = jnp.where(half_lo, rolled[top], d[bot]).astype(bf)
                give(2 * pair, p)
                give(2 * pair + 1, p)

        part(0)
        part(1)

    def to_sibling(ct):
        return send(p1.at[ct], rs1.at[ct], rs1_s.at[ct], rs1_r.at[ct], dev(seg, sib, sec))

    def to_chip(ct, k):
        other = lax.rem(y + k, n_y)
        return send(p2.at[ct, k], rs2.at[ct, k], rs2_s.at[k, ct], rs2_r.at[k, ct], dev(seg, 2 * other + c, sec))

    def mix_in(ct, j):
        part = mixb.at[j, span(ct)]
        return send(part, part, mix_s.at[0], mix_r.at[j, ct], dev(seg, sib, sec))

    def columns(head):
        return pl.ds(pl.multiple_of(head * cols, 128), cols)

    def combine_role():
        load_out.wait()

        def multiply(ct):
            for j in range(heads):
                mix_in(ct, j).wait_recv()
            pairs = [mixb[2 * i, span(ct)] + mixb[2 * i + 1, span(ct)] for i in range(heads // 2)]
            mixture = jnp.concatenate(pairs, axis=1)
            for k in range(n_y):
                other = lax.rem(y + k, n_y)
                p1[ct, k] = dot(mixture, outw[:, columns(2 * other + 1 - c)]).astype(bf)
            to_sibling(ct).start()
            for k in range(n_y):
                other = lax.rem(y + k, n_y)
                p2f[ct, k] = dot(mixture, outw[:, columns(2 * other + c)])

        def reduce(ct):
            to_sibling(ct).wait_recv()
            for k in (1, 3, 2):
                p2[ct, k] = (p2f[ct, k] + rs1[ct, k].astype(f32)).astype(bf)
                to_chip(ct, k).start()

        def finish(t, _):
            ct = done_order(t)
            acc = p2f[ct, 0] + rs1[ct, 0].astype(f32)
            for k in (1, 3, 2):
                to_chip(ct, k).wait_recv()
                acc = acc + rs2[ct, k].astype(f32)
            panel[0, span(ct)] = (hbuf[hd, span(ct)].astype(f32) + acc).astype(bf)

            @pl.when(sec == 0)
            def _():
                hop(ct).start()

            return 0

        def two(t, _):
            @pl.when(t < chunks)
            def _():
                multiply(done_order(t))

            @pl.when(t > 0)
            def _():
                reduce(done_order(t - 1))

            return 0

        lax.fori_loop(0, chunks + 1, two, 0)
        lax.fori_loop(0, chunks, finish, 0)

    def at(i):
        return i + c * (nb - 1 - 2 * i)

    def number(g):
        return g + c * (n_seg - 1 - 2 * g)

    def three(g):
        return xl.at[pl.ds(number(g) * chunks, chunks)]

    def forward(g):
        return send(three(g), three(g), fw_s.at[g], fw_r.at[number(g)], dev(seg, sib, sec))

    def landed(g):
        send(three(g), three(g), fw_s.at[0], fw_r.at[number(g)], dev(seg, sib, sec)).wait_recv()

    def came(g, p):
        turned = lax.rem(c + sec, 2)
        begin = (turned * (chunks - 1), 1 - turned)[p]
        here = xl.at[pl.ds(number(g) * chunks + begin, part_size[p])]
        send(here, here, fw_s.at[0], ch_r.at[number(g), p], dev(seg, sib, sec)).wait_recv()

    def exchange(g):
        return send(exs.at[g], exl.at[g], ex_s.at[g], ex_r.at[g], dev(seg, sib, sec))

    def give_back(i):
        b = at(i)
        return send(
            mxs.at[i - half], mixb.at[mine, span(lax.rem(b, chunks))], mix_s.at[i - half],
            mix_r.at[mine, lax.rem(b, chunks)], dev(b // chunks, 2 * y + cg, sec),
        )

    def chain_role():
        ub[...] = jnp.zeros_like(ub)

        @pl.when(jnp.logical_not(holder))
        def _():
            init_send.wait_recv()

        u[...] = ini[0:64]
        ub[64:128] = ini[0:64].astype(bf)
        w0 = jnp.concatenate([jnp.zeros((128, 64), f32), jnp.swapaxes(ini[64:128], 0, 1)], axis=1)
        w[...] = w0
        wk[...] = w0.astype(bf)
        sc = ini[128:129]
        came(0, 0)

        @pl.when(sec == 1)
        def _():
            came(0, 1)
            forward(0).start()


        z = dot(xl[at(0), 0:64], ub[0:128])

        def mixed(m, t, mine_out):
            i = chunks * m + t - 1
            slot = nb + 1 - chunks * m - t
            both = mine_out + exl[slot // chunks, lax.rem(slot, chunks)]
            both = jnp.where(lo, 0.0, both)
            both = jnp.where(lax.rem(mine, 2) == 0, pltpu.roll(both, 64, 1), both)
            mxs[i - half] = both.astype(bf)
            give_back(i).start()

        def group(g, carry):
            ahead = jnp.where(sec == 1, 0, line // 2 - 1)

            @pl.when(jnp.logical_and(g <= ahead, sec == 0))
            def _():
                came(g, 1)
                forward(g).start()

            @pl.when(g < line - 1)
            def _():
                came(g + 1, 0)

            @pl.when(jnp.logical_and(g >= ahead, g < line - 1))
            def _():
                came(g + 1, 1)
                forward(g + 1).start()

            @pl.when(jnp.logical_and(g >= line - 1, g < n_seg - 1))
            def _():
                landed(g + 1)

            z, back = carry
            for t in range(chunks):
                i = chunks * g + t
                before, after = jnp.maximum(i - 1, 0), jnp.minimum(i + 1, nb - 1)
                z, back, out = chain_step(xl, at(before), at(i), at(after), z, back, sc, u, w, ub, wk)
                exs[g, t] = out

            @pl.when(g <= line)
            def _():
                exchange(g).start()

            @pl.when(g > line)
            def _():
                m = g - 1

                @pl.when(m == line)
                def _():
                    exchange(line).wait_recv()

                exchange(n_seg - 1 - m).wait_recv()

                @pl.when(m > line)
                def _():
                    mixed(m, 0, exs[m, 0])

                for t in range(1, chunks):
                    mixed(m, t, exs[m, t])

            return z, back

        carry = lax.fori_loop(0, n_seg, group, (z, jnp.zeros((64, 128), bf)))
        exchange(0).wait_recv()
        for t in range(chunks):
            mixed(n_seg - 1, t, exs[n_seg - 1, t])
        last = xl[at(nb - 1), 0:64]
        ub[64:128] = (u[...] - dot_tn(last, carry[1])[64:128]).astype(bf)
        aq = smooth(dot(last, ub[64:192])).astype(bf)
        mixed(n_seg, 0, pltpu.roll(last.astype(f32), 64, 1) + dot(aq, wk[...]))

    def chain_drain():
        def drain(i, _):
            give_back(half + i).wait_send()
            return 0

        lax.fori_loop(0, half, drain, 0)
        for g in range(line):
            forward(g).wait_send()
        for g in range(line + 1):
            exchange(g).wait_send()

    project_role()

    @pl.when(in_chain)
    def _():
        chain_role()

    combine_role()

    def drain(ct, _):
        for k in range(n_y):
            pass_on(ct, k).wait_send()
        for k in range(1, n_y):
            direct(ct, k).wait_send()
            to_chip(ct, k).wait_send()
        to_sibling(ct).wait_send()

        @pl.when(sec == 0)
        def _():
            hop(ct).wait_send()

        return 0

    lax.fori_loop(0, chunks, drain, 0)

    @pl.when(in_chain)
    def _():
        chain_drain()

    for j in range(heads):

        @pl.when(jnp.logical_not(jnp.logical_and(holder, mine == j)))
        def _():
            for p in range(2):
                push(j, p).wait_send()

    @pl.when(holder)
    def _():
        init_send.wait_send()


def solution(mesh):
    n_seg, n_head = mesh.shape["seg"], mesh.shape["head"]
    placed = (
        P("seg", "head"),
        P("section", None, None, "head"),
        P("section", "head", None),
        P("section", None, "head", None, None),
        P("section", None, "head", None, None),
        P("section", None, "head"),
        P("seg"),
    )

    def local(tokens, in_weight, out_weight, expand_init, contract_init, inner_rate, seg_counts):
        rows, cols = tokens.shape
        heads = expand_init.shape[2]
        chunks = rows // MB
        nb = n_seg * chunks
        n_y = n_head // 2
        any_space = pl.BlockSpec(memory_space=pltpu.HBM)
        vmem = pl.BlockSpec(memory_space=pltpu.VMEM)
        smem = pl.BlockSpec(memory_space=pltpu.SMEM)
        dma = pltpu.SemaphoreType.DMA
        return pl.pallas_call(
            functools.partial(kernel, n_seg, n_head, heads),
            out_shape=jax.ShapeDtypeStruct((1, rows, cols), bf),
            in_specs=[any_space] * 5 + [smem, smem],
            out_specs=vmem,
            scratch_shapes=[
                pltpu.VMEM(in_weight.shape[1:], bf),
                pltpu.VMEM(out_weight.shape[1:], bf),
                pltpu.VMEM((n_head, rows, cols), bf),
                pltpu.VMEM((3, rows, cols), f32),
                pltpu.VMEM((heads, chunks, 96, 128), bf),
                pltpu.VMEM((nb, 96, 128), bf),
                pltpu.VMEM((136, 128), f32),
                pltpu.VMEM((136, 128), f32),
                pltpu.VMEM((n_seg, chunks, 64, 128), f32),
                pltpu.VMEM((n_seg // 2 + 1, chunks, 64, 128), f32),
                pltpu.VMEM((nb // 2, 64, 128), bf),
                pltpu.VMEM((heads, rows, 128), bf),
                pltpu.VMEM((chunks, n_y, MB, cols), bf),
                pltpu.VMEM((chunks, n_y, MB, cols), f32),
                pltpu.VMEM((chunks, n_y, MB, cols), bf),
                pltpu.VMEM((chunks, n_y, MB, cols), bf),
                pltpu.VMEM((chunks, n_y, MB, cols), bf),
                pltpu.VMEM((64, 128), f32),
                pltpu.VMEM((128, 128), f32),
                pltpu.VMEM((192, 128), bf),
                pltpu.VMEM((128, 128), bf),
                dma((2,)),
                dma,
                dma((4,)),
                dma((n_y, chunks)),
                dma((n_head, chunks)),
                dma((n_y, chunks)),
                dma((chunks,)),
                dma((heads, 2)),
                dma((n_seg, 2)),
                dma((n_seg // 2,)),
                dma((n_seg,)),
                dma((n_seg // 2 + 1,)),
                dma((n_seg // 2 + 1,)),
                dma((nb // 2,)),
                dma((heads, chunks)),
                dma((chunks,)),
                dma((chunks,)),
                dma((n_y, chunks)),
                dma((n_y, chunks)),
                dma,
                dma,
            ],
            compiler_params=pltpu.CompilerParams(
                collective_id=0, has_side_effects=True, vmem_limit_bytes=55009 << 10
            ),
            name="both_groups",
        )(tokens, in_weight, out_weight, expand_init, jnp.swapaxes(contract_init, 3, 4), inner_rate, seg_counts)

    return jax.shard_map(
        local, mesh=mesh, in_specs=placed, out_specs=P("section", "seg", "head"), check_vma=False
    )
```

```python
import functools
import math

import jax
import jax.numpy as jnp
from jax import lax
from jax.experimental import pallas as pl
from jax.experimental.pallas import tpu as pltpu
from jax.sharding import PartitionSpec as P

MB = 64
C1 = math.sqrt(2.0 / math.pi)
C3 = 0.044715
f32 = jnp.float32
bf = jnp.bfloat16


def dot(a, b):
    return lax.dot_general(a, b, (((1,), (0,)), ((), ())), preferred_element_type=f32)


def dot_nt(a, b):
    return lax.dot_general(a, b, (((1,), (1,)), ((), ())), preferred_element_type=f32)


def dot_tn(a, b):
    return lax.dot_general(a, b, (((0,), (0,)), ((), ())), preferred_element_type=f32)


def smooth(z):
    t = jnp.tanh(z * (C1 + (C1 * C3) * (z * z)))
    h = 0.5 * z
    return h + h * t


def smooth_slope(z):
    z2 = z * z
    t = jnp.tanh(z * (C1 + (C1 * C3) * z2))
    h = 0.5 * z
    return h + h * t, 0.5 + 0.5 * t + h * (1.0 - t * t) * (C1 + (3.0 * C1 * C3) * z2)


def chain_step(xl, bp, b, bn, z, bk, sc, u, w, ub, wk):
    xp, xb, xn = xl[bp, 0:64], xl[b, 0:64], xl[bn, 0:64]
    dp = xl[b, 64:96].astype(f32)
    hi = lax.broadcasted_iota(jnp.int32, (64, 128), 1) >= 64
    a, s = smooth_slope(z)
    s = s * sc
    ab = a.astype(bf)
    wkv = wk[...]
    delta = jnp.where(hi, jnp.concatenate([pltpu.roll(dp, 64, 1), dp], 0), 0.0)
    e = delta + dot(ab, wkv)
    back = (dot_nt(e.astype(bf), wkv) * s).astype(bf)
    un = u[...] - dot_tn(xp, bk)[64:128]
    u[...] = un
    ub[64:128] = un.astype(bf)
    zq = dot(xp, ub[64:192])
    gram = dot_nt(jnp.where(hi, xn, jnp.zeros_like(xn)), xb).astype(bf)
    zn = dot(xn, ub[0:128]) - dot(gram, back)
    aq = smooth(zq).astype(bf)
    out = pltpu.roll(xp.astype(f32), 64, 1) + dot(aq, wkv)
    wn = w[...] - dot_tn(ab, (e * sc).astype(bf))
    w[...] = wn
    wk[...] = wn.astype(bf)
    return zn, back, out


def kernel(
    n_seg, n_head, heads,
    tokens, in_w, out_w, expand, contract, rate, counts,
    panel,
    inw, outw, hbuf, acc, stg, xl, ini_s, ini, exs, exl, mxs, mixb,
    p1, p2f, rs1, p2, rs2, u, w, ub, wk,
    wsem, tsem, isem, ag_s, ag_r, po_s, hop_s, push_s, ch_r, fw_s, fw_r, ex_s, ex_r,
    mix_s, mix_r, rs1_s, rs1_r, rs2_s, rs2_r, ini_ss, ini_r, go,
):
    rows = tokens.shape[0]
    cols = tokens.shape[1]
    chunks = rows // MB
    nb = n_seg * chunks
    half = nb // 2
    n_y = n_head // 2
    line = n_seg // 2
    turn_by = line // 2 + 1
    sec = lax.axis_index("section")
    seg = lax.axis_index("seg")
    hd = lax.axis_index("head")
    y = hd // 2
    c = lax.rem(hd, 2)
    sib = 2 * y + 1 - c
    late = seg // line
    from_end = seg + late * (n_seg - 1 - 2 * seg)
    spot = lax.rem(lax.rem(seg, line) + line - turn_by, line)
    in_chain = spot < heads
    cg = late
    mine = jnp.minimum(spot, heads - 1)

    def mirror(f):
        return f + late * (n_seg - 1 - 2 * f)

    waves = ((1, (2, 3)), (3, (4, 5, 6, 7)))

    def place(group, j):
        return group * line + lax.rem(j + turn_by, line)

    holder = jnp.logical_and(in_chain, cg == c)

    def dev(s, h, x):
        return {"seg": s, "head": h, "section": x}

    def send(src, dst, s_sem, r_sem, device):
        return pltpu.make_async_remote_copy(
            src_ref=src, dst_ref=dst, send_sem=s_sem, recv_sem=r_sem,
            device_id=device, device_id_type=pl.DeviceIdType.MESH,
        )

    def span(ct):
        return pl.ds(pl.multiple_of(ct * MB, MB), MB)

    load_in = pltpu.make_async_copy(in_w.at[0], inw, wsem.at[0])
    load_out = pltpu.make_async_copy(out_w.at[0], outw, wsem.at[1])
    load_tok = pltpu.make_async_copy(tokens, hbuf.at[hd], tsem)

    @pl.when(sec == 0)
    def _():
        load_tok.start()

    load_in.start()
    load_out.start()

    barrier = pltpu.get_barrier_semaphore()

    def greet(device):
        pl.semaphore_signal(barrier, inc=1, device_id=device, device_id_type=pl.DeviceIdType.MESH)

    for j in range(heads):
        greet(dev(place(c, j), 2 * y + 1 - late, sec))

    @pl.when(in_chain)
    def _():
        for k in range(line):
            source = c * line + k

            @pl.when(jnp.logical_not(jnp.logical_and(holder, source == seg)))
            def _():
                greet(dev(source, 2 * y + cg, sec))

    for leader, followers in waves:
        for follower in followers:

            @pl.when(from_end == follower)
            def _():
                greet(dev(mirror(leader), hd, sec))

    @pl.when(sec == 1)
    def _():
        greet(dev(seg, hd, 0))

    for k in range(1, n_head):
        greet(dev(seg, lax.rem(hd + k, n_head), sec))

    @pl.when(holder)
    def _():
        loads = []
        for way, to in ((c, ini), (1 - c, ini_s)):
            loads.append(pltpu.make_async_copy(expand.at[0, way, mine], to.at[pl.ds(0, 64)], isem.at[len(loads)]))
            loads.append(pltpu.make_async_copy(contract.at[0, way, mine], to.at[pl.ds(64, 64)], isem.at[len(loads)]))
        for copy in loads:
            copy.start()
        for way, to in ((c, ini), (1 - c, ini_s)):
            to[128:136] = jnp.full((8, 128), rate[0, way, mine] * (1.0 / (64 * MB)), f32)
        for copy in loads:
            copy.wait()

    @pl.when(sec == 0)
    def _():
        load_tok.wait()

    total = n_head - 1 + heads + (1 - sec)
    total = total + jnp.where(in_chain, line, 0) - jnp.where(holder, 1, 0)
    for leader, followers in waves:
        total = total + jnp.where(from_end == leader, len(followers), 0)
    pl.semaphore_wait(barrier, total)

    def direct(ct, k):
        part = hbuf.at[hd, span(ct)]
        return send(part, part, ag_s.at[k, ct], ag_r.at[hd, ct], dev(seg, 2 * lax.rem(y + k, n_y) + c, sec))

    def hop(ct):
        return send(panel.at[0, span(ct)], hbuf.at[hd, span(ct)], hop_s.at[ct], ag_r.at[hd, ct], dev(seg, hd, 1))

    def pass_on(ct, k):
        slot = 2 * lax.rem(y + k, n_y) + c
        part = hbuf.at[slot, span(ct)]
        return send(part, part, po_s.at[k, ct], ag_r.at[slot, ct], dev(seg, sib, sec))

    def arrived(slot, ct):
        part = hbuf.at[slot, span(ct)]
        send(part, part, po_s.at[0, ct], ag_r.at[slot, ct], dev(seg, sib, sec)).wait_recv()

    flip = lax.rem(late + sec, 2)

    def need_order(t):
        return t + flip * (chunks - 1 - 2 * t)

    def done_order(t):
        return t + (1 - late) * (chunks - 1 - 2 * t)

    @pl.when(sec == 0)
    def _():
        def go(t, _):
            for k in (2, 1, 3):
                direct(need_order(t), k).start()
            return 0

        lax.fori_loop(0, chunks, go, 0)

    init_send = send(ini_s, ini, ini_ss, ini_r, dev(seg, sib, sec))

    @pl.when(holder)
    def _():
        init_send.start()

    part_first = (flip * (chunks - 1), 1 - flip)
    part_size = (1, chunks - 1)

    def block(p):
        return pl.ds(seg * chunks + part_first[p], part_size[p])

    def push(j, p):
        return send(
            stg.at[j, pl.ds(part_first[p], part_size[p])], xl.at[block(p)], push_s.at[j, p], ch_r.at[seg, p],
            dev(place(c, j), 2 * y + late, sec),
        )

    def give(j, p):
        own = jnp.logical_and(holder, mine == j)

        @pl.when(own)
        def _():
            pltpu.make_async_copy(
                stg.at[j, pl.ds(part_first[p], part_size[p])], xl.at[block(p)], ch_r.at[seg, p]
            ).start()

        @pl.when(jnp.logical_not(own))
        def _():
            push(j, p).start()

    lo = lax.broadcasted_iota(jnp.int32, (MB, 128), 1) < 64

    def project_role():
        io0 = lax.broadcasted_iota(jnp.int32, (128, 128), 0) // 64
        io1 = lax.broadcasted_iota(jnp.int32, (128, 128), 1) // 64
        ones = jnp.where(io0 == io1, 1.0 / 64, 0.0).astype(bf)

        def unit_rows(x):
            x = x.astype(bf).astype(f32)
            sq = x * x
            top = sq.astype(bf)
            low = (sq - top.astype(f32)).astype(bf)
            return x * lax.rsqrt(dot(top, ones) + dot(low, ones) + 1e-06)

        def spread(t, _):
            ct = need_order(t)

            @pl.when(sec == 1)
            def _():
                arrived(hd, ct)
                for k in (2, 1, 3):
                    direct(ct, k).start()

            pass_on(ct, 0).start()
            return 0

        def relay(t, _):
            ct = need_order(t)
            for k in (1, 3, 2):
                arrived(2 * lax.rem(y + k, n_y) + c, ct)
                pass_on(ct, k).start()
            return 0

        def lead(which):
            leader, followers = waves[which]

            @pl.when(from_end == leader)
            def _():
                for follower in followers:
                    pl.semaphore_signal(
                        go, inc=1, device_id=dev(mirror(follower), hd, sec), device_id_type=pl.DeviceIdType.MESH
                    )

        def part(p):
            times = (0, 1) if p == 0 else (1, chunks)
            size = part_size[p] * MB
            begin = pl.multiple_of(part_first[p] * MB, MB)
            span_p = pl.ds(begin, size)

            def add(k):
                chip = lax.rem(y + k, n_y)

                def await_one(t, _):
                    arrived(2 * chip + 1 - c, need_order(t))
                    return 0

                lax.fori_loop(*times, await_one, 0)
                h = jnp.concatenate([hbuf[2 * chip, span_p], hbuf[2 * chip + 1, span_p]], axis=1)
                at = pl.ds(pl.multiple_of(chip * 2 * cols, 128), 2 * cols)
                for i in range(3):
                    term = dot(h, inw[i, at])
                    acc[i, 0:size] = term if k == 0 else acc[i, 0:size] + term

            if p == 0:
                lax.fori_loop(0, chunks, spread, 0)
                load_in.wait()
                add(0)
                relay(0, 0)
            else:
                relay(1, 0)
                add(0)
                lax.fori_loop(2, chunks, relay, 0)
            for k in (1, 3, 2):
                add(k)
            if p == 1:
                lead(0)
            live = lax.broadcasted_iota(jnp.int32, (size, 128), 0) + begin < counts[0]
            lo_all = lax.broadcasted_iota(jnp.int32, (size, 128), 1) < 64
            for pair in range(heads // 2):
                at = slice(pair * 128, pair * 128 + 128)
                q = unit_rows(acc[0, 0:size, at])
                k = unit_rows(acc[1, 0:size, at])
                v = unit_rows(acc[2, 0:size, at])
                d = jnp.where(live, k - v, 0.0)
                k = jnp.where(live, k, 0.0)
                rolled = pltpu.roll(d, 64, 1)
                even = jnp.where(lo_all, q, pltpu.roll(k, 64, 1)).astype(bf)
                odd = jnp.where(lo_all, pltpu.roll(q, 64, 1), k).astype(bf)
                half_lo = lo[0 : MB // 2]
                for n in range(part_size[p]):
                    ct = part_first[p] + n
                    top = slice(n * MB, n * MB + MB // 2)
                    bot = slice(n * MB + MB // 2, n * MB + MB)
                    stg[2 * pair, ct, 0:64] = even[n * MB : n * MB + MB]
                    stg[2 * pair, ct, 64:96] = jnp.where(half_lo, d[top], rolled[bot]).astype(bf)
                    stg[2 * pair + 1, ct, 0:64] = odd[n * MB : n * MB + MB]
                    stg[2 * pair + 1, ct, 64:96] = jnp.where(half_lo, rolled[top], d[bot]).astype(bf)
                if p == 0:
                    give(2 * pair, p)
                    give(2 * pair + 1, p)
                else:

                    @pl.when(from_end < 2)
                    def _():
                        give(2 * pair, p)
                        give(2 * pair + 1, p)


        part(0)
        part(1)

        @pl.when(from_end >= 2)
        def _():
            pl.semaphore_wait(go, 1)
            lead(1)
            for j in range(heads):
                give(j, 1)

    def to_sibling(ct):
        return send(p1.at[ct], rs1.at[ct], rs1_s.at[ct], rs1_r.at[ct], dev(seg, sib, sec))

    def to_chip(ct, k):
        other = lax.rem(y + k, n_y)
        return send(p2.at[ct, k], rs2.at[ct, k], rs2_s.at[k, ct], rs2_r.at[k, ct], dev(seg, 2 * other + c, sec))

    def mix_in(ct, j):
        part = mixb.at[j, span(ct)]
        return send(part, part, mix_s.at[0], mix_r.at[j, ct], dev(seg, sib, sec))

    def columns(head):
        return pl.ds(pl.multiple_of(head * cols, 128), cols)

    def combine_role():
        load_out.wait()

        def multiply(ct):
            for j in range(heads):
                mix_in(ct, j).wait_recv()
            pairs = [mixb[2 * i, span(ct)] + mixb[2 * i + 1, span(ct)] for i in range(heads // 2)]
            mixture = jnp.concatenate(pairs, axis=1)
            for k in range(n_y):
                other = lax.rem(y + k, n_y)
                p1[ct, k] = dot(mixture, outw[:, columns(2 * other + 1 - c)]).astype(bf)
            to_sibling(ct).start()
            for k in range(n_y):
                other = lax.rem(y + k, n_y)
                p2f[ct, k] = dot(mixture, outw[:, columns(2 * other + c)])

        def reduce(ct):
            to_sibling(ct).wait_recv()
            for k in (1, 3, 2):
                p2[ct, k] = (p2f[ct, k] + rs1[ct, k].astype(f32)).astype(bf)
                to_chip(ct, k).start()

        def finish(t, _):
            ct = done_order(t)
            acc = p2f[ct, 0] + rs1[ct, 0].astype(f32)
            for k in (1, 3, 2):
                to_chip(ct, k).wait_recv()
                acc = acc + rs2[ct, k].astype(f32)
            panel[0, span(ct)] = (hbuf[hd, span(ct)].astype(f32) + acc).astype(bf)

            @pl.when(sec == 0)
            def _():
                hop(ct).start()

            return 0

        def two(t, _):
            @pl.when(t < chunks)
            def _():
                multiply(done_order(t))

            @pl.when(t > 0)
            def _():
                reduce(done_order(t - 1))

            return 0

        lax.fori_loop(0, chunks + 1, two, 0)
        lax.fori_loop(0, chunks, finish, 0)

    def at(i):
        return i + c * (nb - 1 - 2 * i)

    def number(g):
        return g + c * (n_seg - 1 - 2 * g)

    def three(g):
        return xl.at[pl.ds(number(g) * chunks, chunks)]

    def forward(g):
        return send(three(g), three(g), fw_s.at[g], fw_r.at[number(g)], dev(seg, sib, sec))

    def landed(g):
        send(three(g), three(g), fw_s.at[0], fw_r.at[number(g)], dev(seg, sib, sec)).wait_recv()

    def came(g, p):
        turned = lax.rem(c + sec, 2)
        begin = (turned * (chunks - 1), 1 - turned)[p]
        here = xl.at[pl.ds(number(g) * chunks + begin, part_size[p])]
        send(here, here, fw_s.at[0], ch_r.at[number(g), p], dev(seg, sib, sec)).wait_recv()

    def exchange(g):
        return send(exs.at[g], exl.at[g], ex_s.at[g], ex_r.at[g], dev(seg, sib, sec))

    def give_back(i):
        b = at(i)
        return send(
            mxs.at[i - half], mixb.at[mine, span(lax.rem(b, chunks))], mix_s.at[i - half],
            mix_r.at[mine, lax.rem(b, chunks)], dev(b // chunks, 2 * y + cg, sec),
        )

    def chain_role():
        ub[...] = jnp.zeros_like(ub)

        @pl.when(jnp.logical_not(holder))
        def _():
            init_send.wait_recv()

        u[...] = ini[0:64]
        ub[64:128] = ini[0:64].astype(bf)
        w0 = jnp.concatenate([jnp.zeros((128, 64), f32), jnp.swapaxes(ini[64:128], 0, 1)], axis=1)
        w[...] = w0
        wk[...] = w0.astype(bf)
        sc = ini[128:129]
        came(0, 0)

        @pl.when(sec == 1)
        def _():
            came(0, 1)
            forward(0).start()


        z = dot(xl[at(0), 0:64], ub[0:128])

        def mixed(m, t, mine_out):
            i = chunks * m + t - 1
            slot = nb + 1 - chunks * m - t
            both = mine_out + exl[slot // chunks, lax.rem(slot, chunks)]
            both = jnp.where(lo, 0.0, both)
            both = jnp.where(lax.rem(mine, 2) == 0, pltpu.roll(both, 64, 1), both)
            mxs[i - half] = both.astype(bf)
            give_back(i).start()

        def group(g, carry):
            ahead = jnp.where(sec == 1, 0, line // 2 - 1)

            @pl.when(jnp.logical_and(g <= ahead, sec == 0))
            def _():
                came(g, 1)
                forward(g).start()

            @pl.when(g < line - 1)
            def _():
                came(g + 1, 0)

            @pl.when(jnp.logical_and(g >= ahead, g < line - 1))
            def _():
                came(g + 1, 1)
                forward(g + 1).start()

            @pl.when(jnp.logical_and(g >= line - 1, g < n_seg - 1))
            def _():
                landed(g + 1)

            z, back = carry
            for t in range(chunks):
                i = chunks * g + t
                before, after = jnp.maximum(i - 1, 0), jnp.minimum(i + 1, nb - 1)
                z, back, out = chain_step(xl, at(before), at(i), at(after), z, back, sc, u, w, ub, wk)
                exs[g, t] = out

            @pl.when(g <= line)
            def _():
                exchange(g).start()

            @pl.when(g > line)
            def _():
                m = g - 1

                @pl.when(m == line)
                def _():
                    exchange(line).wait_recv()

                exchange(n_seg - 1 - m).wait_recv()

                @pl.when(m > line)
                def _():
                    mixed(m, 0, exs[m, 0])

                for t in range(1, chunks):
                    mixed(m, t, exs[m, t])

            return z, back

        carry = lax.fori_loop(0, n_seg, group, (z, jnp.zeros((64, 128), bf)))
        exchange(0).wait_recv()
        for t in range(chunks):
            mixed(n_seg - 1, t, exs[n_seg - 1, t])
        last = xl[at(nb - 1), 0:64]
        ub[64:128] = (u[...] - dot_tn(last, carry[1])[64:128]).astype(bf)
        aq = smooth(dot(last, ub[64:192])).astype(bf)
        mixed(n_seg, 0, pltpu.roll(last.astype(f32), 64, 1) + dot(aq, wk[...]))

    def chain_drain():
        def drain(i, _):
            give_back(half + i).wait_send()
            return 0

        lax.fori_loop(0, half, drain, 0)
        for g in range(line):
            forward(g).wait_send()
        for g in range(line + 1):
            exchange(g).wait_send()

    project_role()

    @pl.when(in_chain)
    def _():
        chain_role()

    combine_role()

    def drain(ct, _):
        for k in range(n_y):
            pass_on(ct, k).wait_send()
        for k in range(1, n_y):
            direct(ct, k).wait_send()
            to_chip(ct, k).wait_send()
        to_sibling(ct).wait_send()

        @pl.when(sec == 0)
        def _():
            hop(ct).wait_send()

        return 0

    lax.fori_loop(0, chunks, drain, 0)

    @pl.when(in_chain)
    def _():
        chain_drain()

    for j in range(heads):

        @pl.when(jnp.logical_not(jnp.logical_and(holder, mine == j)))
        def _():
            for p in range(2):
                push(j, p).wait_send()

    @pl.when(holder)
    def _():
        init_send.wait_send()


def solution(mesh):
    n_seg, n_head = mesh.shape["seg"], mesh.shape["head"]
    placed = (
        P("seg", "head"),
        P("section", None, None, "head"),
        P("section", "head", None),
        P("section", None, "head", None, None),
        P("section", None, "head", None, None),
        P("section", None, "head"),
        P("seg"),
    )

    def local(tokens, in_weight, out_weight, expand_init, contract_init, inner_rate, seg_counts):
        rows, cols = tokens.shape
        heads = expand_init.shape[2]
        chunks = rows // MB
        nb = n_seg * chunks
        n_y = n_head // 2
        any_space = pl.BlockSpec(memory_space=pltpu.HBM)
        vmem = pl.BlockSpec(memory_space=pltpu.VMEM)
        smem = pl.BlockSpec(memory_space=pltpu.SMEM)
        dma = pltpu.SemaphoreType.DMA
        return pl.pallas_call(
            functools.partial(kernel, n_seg, n_head, heads),
            out_shape=jax.ShapeDtypeStruct((1, rows, cols), bf),
            in_specs=[any_space] * 5 + [smem, smem],
            out_specs=vmem,
            scratch_shapes=[
                pltpu.VMEM(in_weight.shape[1:], bf),
                pltpu.VMEM(out_weight.shape[1:], bf),
                pltpu.VMEM((n_head, rows, cols), bf),
                pltpu.VMEM((3, rows, cols), f32),
                pltpu.VMEM((heads, chunks, 96, 128), bf),
                pltpu.VMEM((nb, 96, 128), bf),
                pltpu.VMEM((136, 128), f32),
                pltpu.VMEM((136, 128), f32),
                pltpu.VMEM((n_seg, chunks, 64, 128), f32),
                pltpu.VMEM((n_seg // 2 + 1, chunks, 64, 128), f32),
                pltpu.VMEM((nb // 2, 64, 128), bf),
                pltpu.VMEM((heads, rows, 128), bf),
                pltpu.VMEM((chunks, n_y, MB, cols), bf),
                pltpu.VMEM((chunks, n_y, MB, cols), f32),
                pltpu.VMEM((chunks, n_y, MB, cols), bf),
                pltpu.VMEM((chunks, n_y, MB, cols), bf),
                pltpu.VMEM((chunks, n_y, MB, cols), bf),
                pltpu.VMEM((64, 128), f32),
                pltpu.VMEM((128, 128), f32),
                pltpu.VMEM((192, 128), bf),
                pltpu.VMEM((128, 128), bf),
                dma((2,)),
                dma,
                dma((4,)),
                dma((n_y, chunks)),
                dma((n_head, chunks)),
                dma((n_y, chunks)),
                dma((chunks,)),
                dma((heads, 2)),
                dma((n_seg, 2)),
                dma((n_seg // 2,)),
                dma((n_seg,)),
                dma((n_seg // 2 + 1,)),
                dma((n_seg // 2 + 1,)),
                dma((nb // 2,)),
                dma((heads, chunks)),
                dma((chunks,)),
                dma((chunks,)),
                dma((n_y, chunks)),
                dma((n_y, chunks)),
                dma,
                dma,
                pltpu.SemaphoreType.REGULAR,
            ],
            compiler_params=pltpu.CompilerParams(
                collective_id=0, has_side_effects=True, vmem_limit_bytes=55009 << 10
            ),
            name="both_groups",
        )(tokens, in_weight, out_weight, expand_init, jnp.swapaxes(contract_init, 3, 4), inner_rate, seg_counts)

    return jax.shard_map(
        local, mesh=mesh, in_specs=placed, out_specs=P("section", "seg", "head"), check_vma=False
    )
```

```python
import functools
import math

import jax
import jax.numpy as jnp
from jax import lax
from jax.experimental import pallas as pl
from jax.experimental.pallas import tpu as pltpu
from jax.sharding import PartitionSpec as P

MB = 64
C1 = math.sqrt(2.0 / math.pi)
C3 = 0.044715
f32 = jnp.float32
bf = jnp.bfloat16


def dot(a, b):
    return lax.dot_general(a, b, (((1,), (0,)), ((), ())), preferred_element_type=f32)


def dot_nt(a, b):
    return lax.dot_general(a, b, (((1,), (1,)), ((), ())), preferred_element_type=f32)


def dot_tn(a, b):
    return lax.dot_general(a, b, (((0,), (0,)), ((), ())), preferred_element_type=f32)


def smooth(z):
    t = jnp.tanh(z * (C1 + (C1 * C3) * (z * z)))
    h = 0.5 * z
    return h + h * t


def smooth_slope(z):
    z2 = z * z
    t = jnp.tanh(z * (C1 + (C1 * C3) * z2))
    h = 0.5 * z
    return h + h * t, 0.5 + 0.5 * t + h * (1.0 - t * t) * (C1 + (3.0 * C1 * C3) * z2)


def chain_step(xl, bp, b, bn, z, bk, sc, u, w, ub, wk):
    xp, xb, xn = xl[bp, 0:64], xl[b, 0:64], xl[bn, 0:64]
    dp = xl[b, 64:96].astype(f32)
    hi = lax.broadcasted_iota(jnp.int32, (64, 128), 1) >= 64
    a, s = smooth_slope(z)
    s = s * sc
    ab = a.astype(bf)
    wkv = wk[...]
    delta = jnp.where(hi, jnp.concatenate([pltpu.roll(dp, 64, 1), dp], 0), 0.0)
    e = delta + dot(ab, wkv)
    back = (dot_nt(e.astype(bf), wkv) * s).astype(bf)
    un = u[...] - dot_tn(xp, bk)[64:128]
    u[...] = un
    ub[64:128] = un.astype(bf)
    zq = dot(xp, ub[64:192])
    gram = dot_nt(jnp.where(hi, xn, jnp.zeros_like(xn)), xb).astype(bf)
    zn = dot(xn, ub[0:128]) - dot(gram, back)
    aq = smooth(zq).astype(bf)
    out = pltpu.roll(xp.astype(f32), 64, 1) + dot(aq, wkv)
    wn = w[...] - dot_tn(ab, (e * sc).astype(bf))
    w[...] = wn
    wk[...] = wn.astype(bf)
    return zn, back, out


def kernel(
    n_seg, n_head, heads,
    tokens, in_w, out_w, expand, contract, rate, counts,
    panel,
    inw, outw, hbuf, acc, stg, xl, ini_s, ini, exs, exl, mxs, mixb,
    p1, p2f, rs1, p2, rs2, u, w, ub, wk,
    wsem, tsem, isem, ag_s, ag_r, po_s, hop_s, push_s, ch_r, fw_s, fw_r, ex_s, ex_r,
    mix_s, mix_r, rs1_s, rs1_r, rs2_s, rs2_r, ini_ss, ini_r, go,
):
    rows = tokens.shape[0]
    cols = tokens.shape[1]
    chunks = rows // MB
    nb = n_seg * chunks
    half = nb // 2
    n_y = n_head // 2
    line = n_seg // 2
    turn_by = line // 2 + 1
    sec = lax.axis_index("section")
    seg = lax.axis_index("seg")
    hd = lax.axis_index("head")
    y = hd // 2
    c = lax.rem(hd, 2)
    sib = 2 * y + 1 - c
    late = seg // line
    from_end = seg + late * (n_seg - 1 - 2 * seg)
    spot = lax.rem(lax.rem(seg, line) + line - turn_by, line)
    in_chain = spot < heads
    cg = late
    mine = jnp.minimum(spot, heads - 1)

    def mirror(f):
        return f + late * (n_seg - 1 - 2 * f)

    waves = ((1, (2, 3)), (3, (4, 5, 6, 7)))

    def place(group, j):
        return group * line + lax.rem(j + turn_by, line)

    holder = jnp.logical_and(in_chain, cg == c)

    def dev(s, h, x):
        return {"seg": s, "head": h, "section": x}

    def send(src, dst, s_sem, r_sem, device):
        return pltpu.make_async_remote_copy(
            src_ref=src, dst_ref=dst, send_sem=s_sem, recv_sem=r_sem,
            device_id=device, device_id_type=pl.DeviceIdType.MESH,
        )

    def span(ct):
        return pl.ds(pl.multiple_of(ct * MB, MB), MB)

    load_in = pltpu.make_async_copy(in_w.at[0], inw, wsem.at[0])
    load_out = pltpu.make_async_copy(out_w.at[0], outw, wsem.at[1])
    load_tok = pltpu.make_async_copy(tokens, hbuf.at[hd], tsem)

    @pl.when(sec == 0)
    def _():
        load_tok.start()

    load_in.start()
    load_out.start()

    barrier = pltpu.get_barrier_semaphore()

    def greet(device):
        pl.semaphore_signal(barrier, inc=1, device_id=device, device_id_type=pl.DeviceIdType.MESH)

    for j in range(heads):
        greet(dev(place(c, j), 2 * y + 1 - late, sec))

    @pl.when(in_chain)
    def _():
        for k in range(line):
            source = c * line + k

            @pl.when(jnp.logical_not(jnp.logical_and(holder, source == seg)))
            def _():
                greet(dev(source, 2 * y + cg, sec))

    for leader, followers in waves:
        for follower in followers:

            @pl.when(from_end == follower)
            def _():
                greet(dev(mirror(leader), hd, sec))

    @pl.when(sec == 1)
    def _():
        greet(dev(seg, hd, 0))

    for k in range(1, n_head):
        greet(dev(seg, lax.rem(hd + k, n_head), sec))

    @pl.when(holder)
    def _():
        loads = []
        for way, to in ((c, ini), (1 - c, ini_s)):
            loads.append(pltpu.make_async_copy(expand.at[0, way, mine], to.at[pl.ds(0, 64)], isem.at[len(loads)]))
            loads.append(pltpu.make_async_copy(contract.at[0, way, mine], to.at[pl.ds(64, 64)], isem.at[len(loads)]))
        for copy in loads:
            copy.start()
        for way, to in ((c, ini), (1 - c, ini_s)):
            to[128:136] = jnp.full((8, 128), rate[0, way, mine] * (1.0 / (64 * MB)), f32)
        for copy in loads:
            copy.wait()

    @pl.when(sec == 0)
    def _():
        load_tok.wait()

    total = n_head - 1 + heads + (1 - sec)
    total = total + jnp.where(in_chain, line, 0) - jnp.where(holder, 1, 0)
    for leader, followers in waves:
        total = total + jnp.where(from_end == leader, len(followers), 0)
    pl.semaphore_wait(barrier, total)

    def direct(ct, k):
        part = hbuf.at[hd, span(ct)]
        return send(part, part, ag_s.at[k, ct], ag_r.at[hd, ct], dev(seg, 2 * lax.rem(y + k, n_y) + c, sec))

    def hop(ct):
        return send(panel.at[0, span(ct)], hbuf.at[hd, span(ct)], hop_s.at[ct], ag_r.at[hd, ct], dev(seg, hd, 1))

    def pass_on(ct, k):
        slot = 2 * lax.rem(y + k, n_y) + c
        part = hbuf.at[slot, span(ct)]
        return send(part, part, po_s.at[k, ct], ag_r.at[slot, ct], dev(seg, sib, sec))

    def arrived(slot, ct):
        part = hbuf.at[slot, span(ct)]
        send(part, part, po_s.at[0, ct], ag_r.at[slot, ct], dev(seg, sib, sec)).wait_recv()

    flip = lax.rem(late + sec, 2)

    def need_order(t):
        return t + flip * (chunks - 1 - 2 * t)

    def done_order(t):
        return t + (1 - late) * (chunks - 1 - 2 * t)

    @pl.when(sec == 0)
    def _():
        def go(t, _):
            for k in (2, 1, 3):
                direct(need_order(t), k).start()
            return 0

        lax.fori_loop(0, chunks, go, 0)

    init_send = send(ini_s, ini, ini_ss, ini_r, dev(seg, sib, sec))

    @pl.when(holder)
    def _():
        init_send.start()

    part_first = (flip * (chunks - 1), 1 - flip)
    part_size = (1, chunks - 1)

    def block(p):
        return pl.ds(seg * chunks + part_first[p], part_size[p])

    def push(j, p):
        return send(
            stg.at[j, pl.ds(part_first[p], part_size[p])], xl.at[block(p)], push_s.at[j, p], ch_r.at[seg, p],
            dev(place(c, j), 2 * y + late, sec),
        )

    def give(j, p):
        own = jnp.logical_and(holder, mine == j)

        @pl.when(own)
        def _():
            pltpu.make_async_copy(
                stg.at[j, pl.ds(part_first[p], part_size[p])], xl.at[block(p)], ch_r.at[seg, p]
            ).start()

        @pl.when(jnp.logical_not(own))
        def _():
            push(j, p).start()

    lo = lax.broadcasted_iota(jnp.int32, (MB, 128), 1) < 64

    def project_role():
        io0 = lax.broadcasted_iota(jnp.int32, (128, 128), 0) // 64
        io1 = lax.broadcasted_iota(jnp.int32, (128, 128), 1) // 64
        ones = jnp.where(io0 == io1, 1.0 / 64, 0.0).astype(bf)

        def unit_rows(x):
            x = x.astype(bf).astype(f32)
            sq = x * x
            top = sq.astype(bf)
            low = (sq - top.astype(f32)).astype(bf)
            return x * lax.rsqrt(dot(top, ones) + dot(low, ones) + 1e-06)

        def spread(t, _):
            ct = need_order(t)

            @pl.when(sec == 1)
            def _():
                arrived(hd, ct)
                for k in (2, 1, 3):
                    direct(ct, k).start()

            pass_on(ct, 0).start()
            return 0

        def relay(t, _):
            ct = need_order(t)
            for k in (1, 3, 2):
                arrived(2 * lax.rem(y + k, n_y) + c, ct)
                pass_on(ct, k).start()
            return 0

        def lead(which):
            leader, followers = waves[which]

            @pl.when(from_end == leader)
            def _():
                for follower in followers:
                    pl.semaphore_signal(
                        go, inc=1, device_id=dev(mirror(follower), hd, sec), device_id_type=pl.DeviceIdType.MESH
                    )

        def part(p):
            times = (0, 1) if p == 0 else (1, chunks)
            size = part_size[p] * MB
            begin = pl.multiple_of(part_first[p] * MB, MB)
            span_p = pl.ds(begin, size)

            def add(k):
                chip = lax.rem(y + k, n_y)

                def await_one(t, _):
                    arrived(2 * chip + 1 - c, need_order(t))
                    return 0

                lax.fori_loop(*times, await_one, 0)
                h = jnp.concatenate([hbuf[2 * chip, span_p], hbuf[2 * chip + 1, span_p]], axis=1)
                at = pl.ds(pl.multiple_of(chip * 2 * cols, 128), 2 * cols)
                for i in range(3):
                    term = dot(h, inw[i, at])
                    acc[i, 0:size] = term if k == 0 else acc[i, 0:size] + term

            if p == 0:
                lax.fori_loop(0, chunks, spread, 0)
                load_in.wait()
                add(0)
                relay(0, 0)
            else:
                relay(1, 0)
                add(0)
                lax.fori_loop(2, chunks, relay, 0)
            for k in (1, 3, 2):
                add(k)
            if p == 1:
                lead(0)
            live = lax.broadcasted_iota(jnp.int32, (size, 128), 0) + begin < counts[0]
            lo_all = lax.broadcasted_iota(jnp.int32, (size, 128), 1) < 64
            for pair in range(heads // 2):
                at = slice(pair * 128, pair * 128 + 128)
                q = unit_rows(acc[0, 0:size, at])
                k = unit_rows(acc[1, 0:size, at])
                v = unit_rows(acc[2, 0:size, at])
                d = jnp.where(live, k - v, 0.0)
                k = jnp.where(live, k, 0.0)
                rolled = pltpu.roll(d, 64, 1)
                even = jnp.where(lo_all, q, pltpu.roll(k, 64, 1)).astype(bf)
                odd = jnp.where(lo_all, pltpu.roll(q, 64, 1), k).astype(bf)
                half_lo = lo[0 : MB // 2]
                for n in range(part_size[p]):
                    ct = part_first[p] + n
                    top = slice(n * MB, n * MB + MB // 2)
                    bot = slice(n * MB + MB // 2, n * MB + MB)
                    stg[2 * pair, ct, 0:64] = even[n * MB : n * MB + MB]
                    stg[2 * pair, ct, 64:96] = jnp.where(half_lo, d[top], rolled[bot]).astype(bf)
                    stg[2 * pair + 1, ct, 0:64] = odd[n * MB : n * MB + MB]
                    stg[2 * pair + 1, ct, 64:96] = jnp.where(half_lo, rolled[top], d[bot]).astype(bf)
                if p == 0:
                    give(2 * pair, p)
                    give(2 * pair + 1, p)
                else:

                    @pl.when(from_end < 2)
                    def _():
                        give(2 * pair, p)
                        give(2 * pair + 1, p)


        part(0)
        part(1)

        @pl.when(from_end >= 2)
        def _():
            pl.semaphore_wait(go, 1)
            lead(1)
            for j in range(heads):
                give(j, 1)

    def to_sibling(ct):
        return send(p1.at[ct], rs1.at[ct], rs1_s.at[ct], rs1_r.at[ct], dev(seg, sib, sec))

    def to_chip(ct, k):
        other = lax.rem(y + k, n_y)
        return send(p2.at[ct, k], rs2.at[ct, k], rs2_s.at[k, ct], rs2_r.at[k, ct], dev(seg, 2 * other + c, sec))

    def mix_in(ct, j):
        part = mixb.at[j, span(ct)]
        return send(part, part, mix_s.at[0], mix_r.at[j, ct], dev(seg, sib, sec))

    def columns(head):
        return pl.ds(pl.multiple_of(head * cols, 128), cols)

    def combine_role():
        load_out.wait()

        def multiply(ct):
            for j in range(heads):
                mix_in(ct, j).wait_recv()
            pairs = [mixb[2 * i, span(ct)] + mixb[2 * i + 1, span(ct)] for i in range(heads // 2)]
            mixture = jnp.concatenate(pairs, axis=1)
            for k in range(n_y):
                other = lax.rem(y + k, n_y)
                p1[ct, k] = dot(mixture, outw[:, columns(2 * other + 1 - c)]).astype(bf)
            to_sibling(ct).start()
            for k in range(n_y):
                other = lax.rem(y + k, n_y)
                p2f[ct, k] = dot(mixture, outw[:, columns(2 * other + c)])

        def reduce(ct):
            to_sibling(ct).wait_recv()
            for k in (2, 1, 3):
                p2[ct, k] = (p2f[ct, k] + rs1[ct, k].astype(f32)).astype(bf)
                to_chip(ct, k).start()

        def finish(t, _):
            ct = done_order(t)
            acc = p2f[ct, 0] + rs1[ct, 0].astype(f32)
            for k in (1, 3, 2):
                to_chip(ct, k).wait_recv()
                acc = acc + rs2[ct, k].astype(f32)
            panel[0, span(ct)] = (hbuf[hd, span(ct)].astype(f32) + acc).astype(bf)

            @pl.when(sec == 0)
            def _():
                hop(ct).start()

            return 0

        def two(t, _):
            @pl.when(t < chunks)
            def _():
                multiply(done_order(t))

            @pl.when(t > 0)
            def _():
                reduce(done_order(t - 1))

            return 0

        lax.fori_loop(0, chunks + 1, two, 0)
        lax.fori_loop(0, chunks, finish, 0)

    def at(i):
        return i + c * (nb - 1 - 2 * i)

    def number(g):
        return g + c * (n_seg - 1 - 2 * g)

    def three(g):
        return xl.at[pl.ds(number(g) * chunks, chunks)]

    def forward(g):
        return send(three(g), three(g), fw_s.at[g], fw_r.at[number(g)], dev(seg, sib, sec))

    def landed(g):
        send(three(g), three(g), fw_s.at[0], fw_r.at[number(g)], dev(seg, sib, sec)).wait_recv()

    def came(g, p):
        turned = lax.rem(c + sec, 2)
        begin = (turned * (chunks - 1), 1 - turned)[p]
        here = xl.at[pl.ds(number(g) * chunks + begin, part_size[p])]
        send(here, here, fw_s.at[0], ch_r.at[number(g), p], dev(seg, sib, sec)).wait_recv()

    def exchange(g):
        return send(exs.at[g], exl.at[g], ex_s.at[g], ex_r.at[g], dev(seg, sib, sec))

    def give_back(i):
        b = at(i)
        return send(
            mxs.at[i - half], mixb.at[mine, span(lax.rem(b, chunks))], mix_s.at[i - half],
            mix_r.at[mine, lax.rem(b, chunks)], dev(b // chunks, 2 * y + cg, sec),
        )

    def chain_role():
        ub[...] = jnp.zeros_like(ub)

        @pl.when(jnp.logical_not(holder))
        def _():
            init_send.wait_recv()

        u[...] = ini[0:64]
        ub[64:128] = ini[0:64].astype(bf)
        w0 = jnp.concatenate([jnp.zeros((128, 64), f32), jnp.swapaxes(ini[64:128], 0, 1)], axis=1)
        w[...] = w0
        wk[...] = w0.astype(bf)
        sc = ini[128:129]
        came(0, 0)

        @pl.when(sec == 1)
        def _():
            came(0, 1)
            forward(0).start()


        z = dot(xl[at(0), 0:64], ub[0:128])

        def mixed(m, t, mine_out):
            i = chunks * m + t - 1
            slot = nb + 1 - chunks * m - t
            both = mine_out + exl[slot // chunks, lax.rem(slot, chunks)]
            both = jnp.where(lo, 0.0, both)
            both = jnp.where(lax.rem(mine, 2) == 0, pltpu.roll(both, 64, 1), both)
            mxs[i - half] = both.astype(bf)
            give_back(i).start()

        def group(g, carry):
            ahead = jnp.where(sec == 1, 0, line // 2 - 1)

            @pl.when(jnp.logical_and(g <= ahead, sec == 0))
            def _():
                came(g, 1)
                forward(g).start()

            @pl.when(g < line - 1)
            def _():
                came(g + 1, 0)

            @pl.when(jnp.logical_and(g >= ahead, g < line - 1))
            def _():
                came(g + 1, 1)
                forward(g + 1).start()

            @pl.when(jnp.logical_and(g >= line - 1, g < n_seg - 1))
            def _():
                landed(g + 1)

            z, back = carry
            for t in range(chunks):
                i = chunks * g + t
                before, after = jnp.maximum(i - 1, 0), jnp.minimum(i + 1, nb - 1)
                z, back, out = chain_step(xl, at(before), at(i), at(after), z, back, sc, u, w, ub, wk)
                exs[g, t] = out

            @pl.when(g <= line)
            def _():
                exchange(g).start()

            @pl.when(g > line)
            def _():
                m = g - 1

                @pl.when(m == line)
                def _():
                    exchange(line).wait_recv()

                exchange(n_seg - 1 - m).wait_recv()

                @pl.when(m > line)
                def _():
                    mixed(m, 0, exs[m, 0])

                for t in range(1, chunks):
                    mixed(m, t, exs[m, t])

            return z, back

        carry = lax.fori_loop(0, n_seg, group, (z, jnp.zeros((64, 128), bf)))
        exchange(0).wait_recv()
        last = xl[at(nb - 1), 0:64]
        ub[64:128] = (u[...] - dot_tn(last, carry[1])[64:128]).astype(bf)
        aq = smooth(dot(last, ub[64:192])).astype(bf)
        mixed(n_seg, 0, pltpu.roll(last.astype(f32), 64, 1) + dot(aq, wk[...]))
        for t in range(chunks):
            mixed(n_seg - 1, chunks - 1 - t, exs[n_seg - 1, chunks - 1 - t])

    def chain_drain():
        def drain(i, _):
            give_back(half + i).wait_send()
            return 0

        lax.fori_loop(0, half, drain, 0)
        for g in range(line):
            forward(g).wait_send()
        for g in range(line + 1):
            exchange(g).wait_send()

    project_role()

    @pl.when(in_chain)
    def _():
        chain_role()

    combine_role()

    def drain(ct, _):
        for k in range(n_y):
            pass_on(ct, k).wait_send()
        for k in range(1, n_y):
            direct(ct, k).wait_send()
            to_chip(ct, k).wait_send()
        to_sibling(ct).wait_send()

        @pl.when(sec == 0)
        def _():
            hop(ct).wait_send()

        return 0

    lax.fori_loop(0, chunks, drain, 0)

    @pl.when(in_chain)
    def _():
        chain_drain()

    for j in range(heads):

        @pl.when(jnp.logical_not(jnp.logical_and(holder, mine == j)))
        def _():
            for p in range(2):
                push(j, p).wait_send()

    @pl.when(holder)
    def _():
        init_send.wait_send()


def solution(mesh):
    n_seg, n_head = mesh.shape["seg"], mesh.shape["head"]
    placed = (
        P("seg", "head"),
        P("section", None, None, "head"),
        P("section", "head", None),
        P("section", None, "head", None, None),
        P("section", None, "head", None, None),
        P("section", None, "head"),
        P("seg"),
    )

    def local(tokens, in_weight, out_weight, expand_init, contract_init, inner_rate, seg_counts):
        rows, cols = tokens.shape
        heads = expand_init.shape[2]
        chunks = rows // MB
        nb = n_seg * chunks
        n_y = n_head // 2
        any_space = pl.BlockSpec(memory_space=pltpu.HBM)
        vmem = pl.BlockSpec(memory_space=pltpu.VMEM)
        smem = pl.BlockSpec(memory_space=pltpu.SMEM)
        dma = pltpu.SemaphoreType.DMA
        return pl.pallas_call(
            functools.partial(kernel, n_seg, n_head, heads),
            out_shape=jax.ShapeDtypeStruct((1, rows, cols), bf),
            in_specs=[any_space] * 5 + [smem, smem],
            out_specs=vmem,
            scratch_shapes=[
                pltpu.VMEM(in_weight.shape[1:], bf),
                pltpu.VMEM(out_weight.shape[1:], bf),
                pltpu.VMEM((n_head, rows, cols), bf),
                pltpu.VMEM((3, rows, cols), f32),
                pltpu.VMEM((heads, chunks, 96, 128), bf),
                pltpu.VMEM((nb, 96, 128), bf),
                pltpu.VMEM((136, 128), f32),
                pltpu.VMEM((136, 128), f32),
                pltpu.VMEM((n_seg, chunks, 64, 128), f32),
                pltpu.VMEM((n_seg // 2 + 1, chunks, 64, 128), f32),
                pltpu.VMEM((nb // 2, 64, 128), bf),
                pltpu.VMEM((heads, rows, 128), bf),
                pltpu.VMEM((chunks, n_y, MB, cols), bf),
                pltpu.VMEM((chunks, n_y, MB, cols), f32),
                pltpu.VMEM((chunks, n_y, MB, cols), bf),
                pltpu.VMEM((chunks, n_y, MB, cols), bf),
                pltpu.VMEM((chunks, n_y, MB, cols), bf),
                pltpu.VMEM((64, 128), f32),
                pltpu.VMEM((128, 128), f32),
                pltpu.VMEM((192, 128), bf),
                pltpu.VMEM((128, 128), bf),
                dma((2,)),
                dma,
                dma((4,)),
                dma((n_y, chunks)),
                dma((n_head, chunks)),
                dma((n_y, chunks)),
                dma((chunks,)),
                dma((heads, 2)),
                dma((n_seg, 2)),
                dma((n_seg // 2,)),
                dma((n_seg,)),
                dma((n_seg // 2 + 1,)),
                dma((n_seg // 2 + 1,)),
                dma((nb // 2,)),
                dma((heads, chunks)),
                dma((chunks,)),
                dma((chunks,)),
                dma((n_y, chunks)),
                dma((n_y, chunks)),
                dma,
                dma,
                pltpu.SemaphoreType.REGULAR,
            ],
            compiler_params=pltpu.CompilerParams(
                collective_id=0, has_side_effects=True, vmem_limit_bytes=55009 << 10
            ),
            name="both_groups",
        )(tokens, in_weight, out_weight, expand_init, jnp.swapaxes(contract_init, 3, 4), inner_rate, seg_counts)

    return jax.shard_map(
        local, mesh=mesh, in_specs=placed, out_specs=P("section", "seg", "head"), check_vma=False
    )
```
